128 devices in a mesh: dp: 8 (over x, y_hi), seq: 16 (over y_lo, z, core).
Axes of the slice: x: 4, y: 4 (y_hi: 2, y_lo: 2; y = y_hi * 2 + y_lo), z: 4, core: 2. Of those that a mesh axis runs over, the one named last changes fastest.
Arguments:
- tokens: int32 [8, 262144], P('dp', 'seq'), may hold values from 0 to 3
- dilation: int32 [8], P('dp'), may hold values from 1 to 16, as said below
- w_stem: bfloat16 [512, 768], replicated, may hold values from -0.5 to 0.5
- conv_w: bfloat16 [5, 4, 192, 192], replicated, may hold values from -0.1875 to 0.1875
- w_query: bfloat16 [768, 768], replicated, may hold values from -3.6084392 to 3.6084392
- w_key: bfloat16 [768, 768], replicated, may hold values from -0.14433757 to 0.14433757
- w_value: bfloat16 [768, 768], replicated, may hold values from -0.21875 to 0.21875
- w_out: bfloat16 [768, 768], replicated, may hold values from -0.21875 to 0.21875
- cotangent: bfloat16 [8, 2048, 768], P('dp', 'seq'), may hold values from -0.046875 to 0.046875
Outputs:
- mixed: bfloat16 [8, 2048, 768], P('dp', 'seq')
- grad_conv: float32 [5, 4, 192, 192], replicated
- grad_query: float32 [768, 768], replicated
- grad_key: float32 [768, 768], replicated
- grad_value: float32 [768, 768], replicated
- grad_out: float32 [768, 768], replicated
The draws below stay inside these ranges and needn't reach their ends.
Inputs may be any that keep to these rules, and one draw needn't show every extreme that they name: Some sequence has dilation 16.
All inputs are finite; a program needn't handle non-finite values.
Results may differ from the reference program's by a relative error of at most 0.04.
The reference program's roundings to bfloat16 on the way count: a program that leaves them out, or rounds other values in their place, can miss the bound.
Values may be sent and summed in bfloat16 or wider, within the bound.
No kernel may reach another device: no remote copies, remote signals or barrier semaphores. Data moves between devices by JAX's collectives and lax.ppermute only.
A program may use at most 192 MiB of HBM per device.

```python
import jax
import jax.numpy as jnp
from jax import lax

C = 768
H = 16
G = 4
KW = 5
BP = 128
DMAX = 16
BIN_DEV = 128
CG = 192
BINS = 2048
SEQS = 8
N_SEQ = 16


def shared_rows(key):
    return jnp.clip(jax.random.normal(key, (C, C), jnp.float32), -3.0, 3.0) * C ** (-0.5)


def draw_dilation(key, part):
    key = jax.random.fold_in(key, 11)
    first_key, second_key = jax.random.split(key)
    spacings = jax.random.randint(first_key, (SEQS,), 1, DMAX + 1)
    where_max = jax.random.randint(second_key, (), 0, SEQS)
    return spacings.at[where_max].set(DMAX).astype(jnp.int32)


def draw_w_key(key, part):
    shared = shared_rows(key)
    return shared.astype(jnp.bfloat16)


def draw_w_query(key, part):
    key = jax.random.fold_in(key, 23)
    own_rows = jnp.clip(jax.random.normal(key, (C, C), jnp.float32), -3.0, 3.0) * C ** (-0.5)
    values_drawn = own_rows
    return values_drawn.astype(jnp.bfloat16)


def plant(entries, stream_key, smallest, largest):
    place = [jax.random.randint(jax.random.fold_in(stream_key, axis), (), 0, length) for axis, length in enumerate(entries.shape)]
    main_axis = entries.shape.index(max(entries.shape))
    next_to = place[:main_axis] + [(place[main_axis] + 1) % entries.shape[main_axis]] + place[main_axis + 1:]
    return entries.at[tuple(place)].set(smallest).at[tuple(next_to)].set(largest)


def block_scale(stream_key, dims, cuts, smallest, largest):
    def one(axis_at, blocks):
        steps = jax.random.uniform(jax.random.fold_in(jax.random.fold_in(stream_key, 6), axis_at), (blocks,), jnp.float32, smallest / len(cuts), largest / len(cuts))
        return jnp.repeat(jnp.exp(steps), dims[axis_at] // blocks).reshape((-1,) + (1,) * (len(dims) - axis_at - 1))

    loudness = one(*cuts[0])
    for cut in cuts[1:]:
        loudness = loudness * one(*cut)
    return loudness


def bell_draw(own_key, dims, deviation, reach, cuts=(), kind=jnp.bfloat16):
    values = deviation * jax.random.normal(own_key, dims, jnp.float32)
    if cuts:
        values = values * block_scale(own_key, dims, cuts, -0.22, 0.18)
    return jnp.clip(values, -reach, reach).astype(kind)


def setup_inputs(seed: int = 0) -> dict:
    streams_of = jax.random.split(jax.random.key(seed), 10)
    return {
        "tokens": plant(jax.random.randint(streams_of[0], (SEQS, BINS * BP), 0, 4), jax.random.fold_in(streams_of[0], 1), 0, 3).astype(jnp.int32),
        "dilation": draw_dilation(jax.random.fold_in(streams_of[9], 71), 0),
        "w_stem": bell_draw(streams_of[2], (4 * BP, C), BP ** -0.5, 0.5),
        "conv_w": bell_draw(streams_of[3], (KW, G, CG, CG), (KW * CG) ** -0.5, 0.1875),
        "w_query": draw_w_query(jax.random.fold_in(streams_of[9], 71), 0),
        "w_key": draw_w_key(jax.random.fold_in(streams_of[9], 71), 0),
        "w_value": bell_draw(streams_of[6], (C, C), C ** -0.5, 0.21875),
        "w_out": bell_draw(streams_of[7], (C, C), C ** -0.5, 0.21875),
        "cotangent": bell_draw(streams_of[8], (SEQS, BINS, C), ((SEQS * BINS) ** -0.5), 0.046875, ((0, 8), (1, 16))),
    }


def stem_rows(letters_in, w_stem):
    alphabet = jnp.arange(4, dtype=jnp.int32)
    hot_table = (letters_in.reshape(BINS, BP)[:, :, None] == alphabet[None, None, :]).astype(jnp.bfloat16)
    return jnp.dot(hot_table.reshape(BINS, BP * 4), w_stem, preferred_element_type=jnp.float32).astype(jnp.bfloat16)

def conv_shifted(embedded, spacing):
    margin = 2 * DMAX
    padded = jnp.pad(embedded, ((margin, margin), (0, 0)))
    pieces = []
    for tap_index in range(KW):
        start = (margin + (tap_index - KW // 2) * spacing).astype(jnp.int32)
        pieces.append(lax.dynamic_slice_in_dim(padded, start, BINS, 0))
    return jnp.stack(pieces)

def probabilities(query, keys):
    score_scale = (C // H) ** (-0.5)
    scores = jnp.dot(query, keys.T, preferred_element_type=jnp.float32) * score_scale
    highest = lax.optimization_barrier(jnp.max(scores, axis=-1, keepdims=True))
    powers = jnp.exp(scores - highest)
    return powers / lax.optimization_barrier(jnp.sum(powers, axis=-1, keepdims=True))

def head_forward(query, keys, values):
    rounded = probabilities(query, keys).astype(jnp.bfloat16)
    return jnp.dot(rounded, values, preferred_element_type=jnp.float32).astype(jnp.bfloat16)

def head_backward(query, keys, values, output, grad_attn):
    score_scale = (C // H) ** (-0.5)
    probs_full = probabilities(query, keys)
    rounded = probs_full.astype(jnp.bfloat16)
    grad_p = jnp.dot(grad_attn, values.T, preferred_element_type=jnp.float32)
    row_dot = lax.optimization_barrier(jnp.sum(grad_attn.astype(jnp.float32) * output.astype(jnp.float32), axis=-1, keepdims=True))
    grad_s = (probs_full * (grad_p - row_dot)).astype(jnp.bfloat16)
    grad_query = (jnp.dot(grad_s, keys, preferred_element_type=jnp.float32) * score_scale).astype(jnp.bfloat16)
    partitioned_rows = grad_s.astype(jnp.float32).reshape(N_SEQ, BIN_DEV, BINS)
    partitioned_probabilities = rounded.astype(jnp.float32).reshape(N_SEQ, BIN_DEV, BINS)
    query_segments = query.astype(jnp.float32).reshape(N_SEQ, BIN_DEV, -1)
    gradient_pieces_split = grad_attn.astype(jnp.float32).reshape(N_SEQ, BIN_DEV, -1)
    key_segments = jnp.einsum('oel,oey->oly', partitioned_rows, query_segments) * score_scale
    value_segments = jnp.einsum('oel,oey->oly', partitioned_probabilities, gradient_pieces_split)
    key_segments = lax.optimization_barrier(key_segments.astype(jnp.bfloat16)).astype(jnp.float32)
    value_segments = lax.optimization_barrier(value_segments.astype(jnp.bfloat16)).astype(jnp.float32)
    grad_keys = lax.optimization_barrier(jnp.sum(key_segments, axis=0)).astype(jnp.bfloat16)
    grad_values = lax.optimization_barrier(jnp.sum(value_segments, axis=0)).astype(jnp.bfloat16)
    return (grad_query, grad_keys, grad_values)

def split_heads(source):
    return source.reshape(BINS, H, C // H).transpose(1, 0, 2)

def join_heads(source):
    return source.transpose(1, 0, 2).reshape(BINS, C)

def branch(letters_in, spacing, grad_branch, w_stem, conv_w, w_query, w_key, w_value, w_out):
    embedded = stem_rows(letters_in, w_stem)
    shifted = conv_shifted(embedded, spacing).astype(jnp.float32).reshape(KW, BINS, G, C // G)
    preact = jnp.einsum('klgi,kgio->lgo', shifted, conv_w.astype(jnp.float32)).reshape(BINS, C)
    hidden = (embedded.astype(jnp.float32) + jax.nn.gelu(preact)).astype(jnp.bfloat16)
    query = jnp.dot(hidden, w_query, preferred_element_type=jnp.float32).astype(jnp.bfloat16)
    key_rows = jnp.dot(hidden, w_key, preferred_element_type=jnp.float32).astype(jnp.bfloat16)
    value_rows = jnp.dot(hidden, w_value, preferred_element_type=jnp.float32).astype(jnp.bfloat16)
    heads_q, heads_k, heads_v = (split_heads(query), split_heads(key_rows), split_heads(value_rows))
    attn_heads = lax.map(lambda inputs: head_forward(inputs[0], inputs[1], inputs[2]), (heads_q, heads_k, heads_v))
    attn = join_heads(attn_heads)
    branch_out = (hidden.astype(jnp.float32) + jnp.dot(attn, w_out, preferred_element_type=jnp.float32)).astype(jnp.bfloat16)
    grad_out_w = jnp.dot(attn.T, grad_branch, preferred_element_type=jnp.float32)
    grad_attn = jnp.dot(grad_branch, w_out.T, preferred_element_type=jnp.float32).astype(jnp.bfloat16)
    back_heads = lax.map(lambda inputs: head_backward(inputs[0], inputs[1], inputs[2], inputs[3], inputs[4]), (heads_q, heads_k, heads_v, attn_heads, split_heads(grad_attn)))
    grad_q_rows = join_heads(back_heads[0])
    grad_k_rows = join_heads(back_heads[1])
    grad_v_rows = join_heads(back_heads[2])
    grad_hidden = grad_branch.astype(jnp.float32)
    grad_hidden = grad_hidden + jnp.dot(grad_q_rows, w_query.T, preferred_element_type=jnp.float32)
    grad_hidden = grad_hidden + jnp.dot(grad_k_rows, w_key.T, preferred_element_type=jnp.float32)
    grad_hidden = grad_hidden + jnp.dot(grad_v_rows, w_value.T, preferred_element_type=jnp.float32)
    unused, pull_back = jax.vjp(jax.nn.gelu, preact)
    grad_pre = pull_back(grad_hidden)[0].astype(jnp.bfloat16)
    grad_conv = jnp.einsum('klgi,lgo->kgio', shifted, grad_pre.astype(jnp.float32).reshape(BINS, G, C // G))
    grad_q_w = jnp.dot(hidden.T, grad_q_rows, preferred_element_type=jnp.float32)
    grad_k_w = jnp.dot(hidden.T, grad_k_rows, preferred_element_type=jnp.float32)
    grad_v_w = jnp.dot(hidden.T, grad_v_rows, preferred_element_type=jnp.float32)
    return (branch_out, (grad_conv, grad_q_w, grad_k_w, grad_v_w, grad_out_w))

def reference(tokens, dilation, w_stem, conv_w, w_query, w_key, w_value, w_out, cotangent):
    weights = (w_stem, conv_w, w_query, w_key, w_value, w_out)

    def advance(totals, inputs):
        letters_in, spacing, grad_seq = inputs
        first_out, first_grads = branch(letters_in, spacing, grad_seq, *weights)
        reverse_codes = 3 - letters_in[::-1]
        second_out, second_grads = branch(reverse_codes, spacing, grad_seq[::-1], *weights)
        mixed_seq = (first_out.astype(jnp.float32) + second_out[::-1].astype(jnp.float32)).astype(jnp.bfloat16)
        totals = jax.tree.map(lambda left, right, extra: left + right + extra, totals, first_grads, second_grads)
        return (totals, mixed_seq)
    start = (jnp.zeros((KW, G, C // G, C // G), jnp.float32), jnp.zeros((C, C), jnp.float32), jnp.zeros((C, C), jnp.float32), jnp.zeros((C, C), jnp.float32), jnp.zeros((C, C), jnp.float32))
    totals, mixed = lax.scan(advance, start, (tokens, dilation, cotangent))
    return (mixed, totals[0], totals[1], totals[2], totals[3], totals[4])
```

```python
import functools
import math

import jax
import jax.numpy as jnp
from jax import lax
from jax.experimental import pallas as pl
from jax.experimental.pallas import tpu as pltpu
from jax.sharding import PartitionSpec as P

H = 16
G = 4
KW = 5
DMAX = 16
MARGIN = 2 * DMAX
C = 768
CG = C // G
HD = C // H
BP = 128
BINS = 2048
ROWS = 256
BLOCKS = BINS // ROWS
PLANES = C // 128
PIECE = BP + HD
SCALE = HD ** (-0.5)
BF = jnp.bfloat16
F32 = jnp.float32
VMEM_LIMIT = 56 * 1024 * 1024
GELU_A = math.sqrt(2.0 / math.pi)
GELU_B = 0.044715
WINDOWS = (0, 1, 3, 4)


def mm(left, right):
    return jnp.dot(left, right, preferred_element_type=F32)


def mm_nt(left, right):
    return lax.dot_general(left, right, (((1,), (1,)), ((), ())), preferred_element_type=F32)


def vmem():
    return pl.BlockSpec(memory_space=pltpu.VMEM)


def smem():
    return pl.BlockSpec(memory_space=pltpu.SMEM)


def params(**extra):
    return pltpu.CompilerParams(vmem_limit_bytes=VMEM_LIMIT, **extra)


def front_kernel(info, pieces, w_stem, conv, hidden, pre_own, emb_own, stem, emb):
    step = info[0]
    core = info[1]
    chip = info[2]
    row = lax.broadcasted_iota(jnp.int32, (4 * BP, 4 * BP), 0)
    col = lax.broadcasted_iota(jnp.int32, (4 * BP, 4 * BP), 1)
    source = 4 * (row & (BP - 1)) + (row >> 7)
    source = jnp.where(core == 1, 4 * BP - 1 - source, source)
    stem[...] = mm((col == source).astype(BF), w_stem[...]).astype(BF)
    edge = jnp.zeros((PLANES, MARGIN, 128), F32)
    emb[:, 0:MARGIN, :] = edge
    emb[:, MARGIN + BINS : MARGIN + BINS + MARGIN, :] = edge

    def embed(block, carry):
        letters = pieces[pl.ds(2 * block, 2), 0:BP, :].astype(F32).reshape(ROWS, BP)
        hot = jnp.concatenate([(letters == float(c)).astype(BF) for c in range(4)], axis=1)
        rows = mm(hot, stem[...]).astype(BF).astype(F32)
        start = pl.multiple_of(MARGIN + block * ROWS, 8)
        for plane in range(PLANES):
            emb[plane, pl.ds(start, ROWS), :] = rows[:, plane * 128 : (plane + 1) * 128]
        return carry

    lax.fori_loop(0, BLOCKS, embed, 0)

    def convolve(block, carry):
        base = MARGIN + block * ROWS
        planes = [
            [
                emb[plane, pl.ds(base + (tap - KW // 2) * step, ROWS), :].astype(BF)
                for tap in range(KW)
            ]
            for plane in range(PLANES)
        ]
        sums = []
        for group in range(G):
            at = WINDOWS[group]
            left = jnp.concatenate(
                [planes[at + half][tap] for tap in range(KW) for half in range(2)], axis=1
            )
            sums.append(mm(left, conv[group]))
        for pair in range(2):
            even, odd = sums[2 * pair], sums[2 * pair + 1]
            thirds = (even[:, :128], even[:, 128:] + odd[:, :128], odd[:, 128:])
            for third in range(3):
                plane = 3 * pair + third
                x = thirds[third]
                lanes = slice(plane * 128, (plane + 1) * 128)

                @pl.when(block == chip)
                def _(x=x, lanes=lanes):
                    pre_own[:, lanes] = x

                th = jnp.tanh(GELU_A * (x + GELU_B * (x * x * x)))
                act = 0.5 * x * (1.0 + th)
                own = emb[plane, pl.ds(pl.multiple_of(base, 8), ROWS), :]
                hidden[pl.ds(pl.multiple_of(block * ROWS, ROWS), ROWS), lanes] = (own + act).astype(BF)
        return carry

    lax.fori_loop(0, BLOCKS, convolve, 0)
    emb_own[...] = emb[:, pl.ds(pl.multiple_of(chip * ROWS, ROWS), ROWS + 2 * MARGIN), :]


def front(info, pieces, w_stem, conv):
    return pl.pallas_call(
        front_kernel,
        out_shape=(
            jax.ShapeDtypeStruct((BINS, C), BF),
            jax.ShapeDtypeStruct((ROWS, C), F32),
            jax.ShapeDtypeStruct((PLANES, ROWS + 2 * MARGIN, 128), F32),
        ),
        in_specs=[smem(), vmem(), vmem(), vmem()],
        out_specs=(vmem(), vmem(), vmem()),
        scratch_shapes=[
            pltpu.VMEM((4 * BP, C), BF),
            pltpu.VMEM((PLANES, BINS + 2 * MARGIN, 128), F32),
        ],
        compiler_params=params(),
        cost_estimate=pl.CostEstimate(flops=2 * 10**10, bytes_accessed=10**7, transcendentals=0),
        name="front",
    )(info, pieces, w_stem, conv)


def heads_kernel(
    hidden, cot, pieces, w_qkv, out, wgrad,
    q_pad, k_nat, v_nat, q_t, k_t, v_t, ga_t, x_t, scores, rounded, kv_sum,
):
    def project(block, carry):
        rows = pl.ds(pl.multiple_of(block * ROWS, ROWS), ROWS)
        y = mm(hidden[rows, :], w_qkv[...]).astype(BF)
        q_pad[rows, :] = y[:, 0:128]
        k_nat[rows, :] = y[:, 128 : 128 + HD]
        v_nat[rows, :] = y[:, 256 : 256 + HD]
        turned = y.astype(F32).T
        q_t[:, rows] = turned[0:HD].astype(BF)
        k_t[:, rows] = turned[128 : 128 + HD].astype(BF)
        v_t[:, rows] = turned[256 : 256 + HD].astype(BF)
        ga_t[:, rows] = jnp.concatenate([pieces[2 * block, BP:, :], pieces[2 * block + 1, BP:, :]], axis=1)
        return carry

    lax.fori_loop(0, BLOCKS, project, 0)
    kv_sum[...] = jnp.zeros_like(kv_sum)

    def attend(block, carry):
        lanes = pl.ds(pl.multiple_of(block * ROWS, ROWS), ROWS)
        qt = q_t[:, lanes]
        gat = ga_t[:, lanes]
        top = None
        for part in range(BLOCKS):
            at = slice(part * ROWS, (part + 1) * ROWS)
            s = mm(k_nat[at, :], qt)
            scores[at, :] = s
            most = jnp.max(s.reshape(ROWS // 8, 8, ROWS), axis=0)
            top = most if top is None else jnp.maximum(top, most)
        top = jnp.max(top, axis=0, keepdims=True)
        total = None
        for part in range(BLOCKS):
            at = slice(part * ROWS, (part + 1) * ROWS)
            e = jnp.exp2((scores[at, :] - top) * (SCALE * math.log2(math.e)))
            scores[at, :] = e
            some = jnp.sum(e.reshape(ROWS // 8, 8, ROWS), axis=0)
            total = some if total is None else total + some
        inverse = 1.0 / jnp.sum(total, axis=0, keepdims=True)
        attn = None
        for part in range(BLOCKS):
            at = slice(part * ROWS, (part + 1) * ROWS)
            pb = (scores[at, :] * inverse).astype(BF)
            rounded[at, :] = pb
            term = mm(v_t[:, at], pb)
            attn = term if attn is None else attn + term
        attn = attn.astype(BF)
        x_t[0:HD, lanes] = attn
        row_dot = jnp.sum(gat.astype(F32) * attn.astype(F32), axis=0, keepdims=True)
        ga_pad = jnp.concatenate(
            [jnp.zeros((HD, ROWS), F32), gat.astype(F32), jnp.zeros((128 - 2 * HD, ROWS), F32)], axis=0
        ).T.astype(BF)
        right = jnp.concatenate([q_pad[lanes, :], ga_pad], axis=0)
        gq = None
        for part in range(BLOCKS):
            at = slice(part * ROWS, (part + 1) * ROWS)
            gp = mm(v_nat[at, :], gat)
            gs = ((scores[at, :] * inverse) * (gp - row_dot)).astype(BF)
            term = mm(k_t[:, at], gs)
            gq = term if gq is None else gq + term
            kv_sum[at, :] += mm(jnp.concatenate([gs, rounded[at, :]], axis=1), right)
        x_t[HD : 2 * HD, lanes] = (gq * SCALE).astype(BF)
        return carry

    lax.fori_loop(0, BLOCKS, attend, 0)

    wgrad[...] = jnp.zeros_like(wgrad)

    def finish(block, carry):
        rows = pl.ds(pl.multiple_of(block * ROWS, ROWS), ROWS)
        turned = kv_sum[rows, :].T
        x_t[2 * HD : 3 * HD, rows] = (turned[0:HD] * SCALE).astype(BF)
        x_t[3 * HD : 4 * HD, rows] = turned[HD : 2 * HD].astype(BF)
        piece = x_t[:, rows]
        out[block] = piece
        wgrad[0:HD, :] += mm(piece[0:HD], cot[rows, :])
        wgrad[HD:, :] += mm(piece[HD:], hidden[rows, :])
        return carry

    lax.fori_loop(0, BLOCKS, finish, 0)


def heads(hidden, cot, pieces, w_qkv):
    return pl.pallas_call(
        heads_kernel,
        out_shape=(
            jax.ShapeDtypeStruct((BLOCKS, 4 * HD, ROWS), BF),
            jax.ShapeDtypeStruct((4 * HD, C), F32),
        ),
        in_specs=[vmem()] * 4,
        out_specs=(vmem(), vmem()),
        scratch_shapes=[
            pltpu.VMEM((BINS, 128), BF),
            pltpu.VMEM((BINS, HD), BF),
            pltpu.VMEM((BINS, HD), BF),
            pltpu.VMEM((HD, BINS), BF),
            pltpu.VMEM((HD, BINS), BF),
            pltpu.VMEM((HD, BINS), BF),
            pltpu.VMEM((HD, BINS), BF),
            pltpu.VMEM((4 * HD, BINS), BF),
            pltpu.VMEM((BINS, ROWS), F32),
            pltpu.VMEM((BINS, ROWS), BF),
            pltpu.VMEM((BINS, 128), F32),
        ],
        compiler_params=params(),
        cost_estimate=pl.CostEstimate(flops=4 * 10**10, bytes_accessed=10**7, transcendentals=0),
        name="heads",
    )(hidden, cot, pieces, w_qkv)


def tail_kernel(
    info, got, hidden, cot, pre, emb, w_query, w_key, w_value, w_out, branch_out, conv_grad
):
    step = info[0]

    def rows_of(which):
        part = got[:, which * HD : (which + 1) * HD, :].reshape(C, ROWS)
        return part.astype(F32).T.astype(BF)

    branch_out[...] = (hidden[...].astype(F32) + mm(rows_of(0), w_out[...])).astype(BF)
    grad = cot[...].astype(F32) + mm_nt(rows_of(1), w_query[...])
    grad = grad + mm_nt(rows_of(2), w_key[...])
    grad = grad + mm_nt(rows_of(3), w_value[...])
    x = pre[...]
    square = x * x
    th = jnp.tanh(GELU_A * (x + GELU_B * (square * x)))
    slope = 0.5 * (1.0 + th) + 0.5 * x * (1.0 - th * th) * (GELU_A * (1.0 + 3.0 * GELU_B * square))
    grad_t = (grad * slope).astype(BF).astype(F32).T.astype(BF)
    low = lax.broadcasted_iota(jnp.int32, (CG, 128), 1) < 64
    for tap in range(KW):
        start = MARGIN + (tap - KW // 2) * step
        planes = [emb[plane, pl.ds(start, ROWS), :].astype(BF) for plane in range(PLANES)]
        for pair in range(2):
            terms = []
            for half in range(2):
                group = 2 * pair + half
                at = WINDOWS[group]
                right = jnp.concatenate([planes[at], planes[at + 1]], axis=1)
                terms.append(mm(grad_t[group * CG : (group + 1) * CG], right))
            even, odd = terms
            thirds = (even[:, :128], jnp.where(low, even[:, 128:], odd[:, :128]), odd[:, 128:])
            for third in range(3):
                plane = 3 * pair + third
                conv_grad[tap * CG : (tap + 1) * CG, plane * 128 : (plane + 1) * 128] = thirds[third].astype(BF)
    conv_grad[KW * CG :, :] = jnp.zeros((64, C), BF)


def tail(info, got, hidden, cot, pre, emb, w_query, w_key, w_value, w_out):
    return pl.pallas_call(
        tail_kernel,
        out_shape=(
            jax.ShapeDtypeStruct((ROWS, C), BF),
            jax.ShapeDtypeStruct((KW * CG + 64, C), BF),
        ),
        in_specs=[smem()] + [vmem()] * 9,
        out_specs=(vmem(), vmem()),
        compiler_params=params(),
        cost_estimate=pl.CostEstimate(flops=5 * 10**9, bytes_accessed=10**7, transcendentals=0),
        name="tail",
    )(info, got, hidden, cot, pre, emb, w_query, w_key, w_value, w_out)


def apart(axis, bit):
    return [(i, i ^ bit) for i in range(lax.axis_size(axis))]


def body(tokens, dilation, w_stem, conv_w, w_query, w_key, w_value, w_out, cotangent):
    me = lax.axis_index("seq")
    core = me & 1
    chip = me >> 1
    step = jnp.where(core == 1, -dilation[0], dilation[0])
    info = jnp.stack([step, core, chip]).astype(jnp.int32)
    own_cot = cotangent[0]
    cot = lax.all_gather(own_cot, "seq", axis=0, tiled=True)
    ga_t = lax.dot_general(w_out, own_cot, (((1,), (1,)), ((), ())), preferred_element_type=F32).astype(BF)
    letters = jnp.broadcast_to(tokens.reshape(1, BP, BP).astype(BF), (H, BP, BP))
    pieces = lax.all_to_all(
        jnp.concatenate([letters, ga_t.reshape(H, HD, BP)], axis=1), "seq", 0, 0, tiled=True
    )
    taps = conv_w.transpose(1, 0, 2, 3)
    conv = jnp.stack(
        [
            jnp.pad(taps[group], ((0, 0), (64, 0), (64, 0)) if group % 2 else ((0, 0), (0, 64), (0, 64)))
            for group in range(G)
        ]
    ).reshape(G, KW * 256, 256)
    w_qkv = jnp.concatenate(
        [
            jnp.pad(lax.dynamic_slice_in_dim(w, me * HD, HD, 1), ((0, 0), (0, 128 - HD)))
            for w in (w_query, w_key, w_value)
        ],
        axis=1,
    )
    hidden, pre_own, emb_own = front(info, pieces, w_stem, conv)
    hidden_other = lax.ppermute(hidden, "seq", apart("seq", 1))
    mine, wgrad_mine = heads(hidden, cot, pieces, w_qkv)
    other, wgrad_other = heads(hidden_other, cot, pieces, w_qkv)
    first = jnp.where(core == 0, mine, other)
    second = jnp.where(core == 0, other, mine)
    got = lax.all_to_all(
        jnp.stack([first, second], axis=1).reshape(H, 4 * HD, ROWS), "seq", 0, 0, tiled=True
    )
    hidden_own = lax.dynamic_slice_in_dim(hidden, chip * ROWS, ROWS, 0)
    cot_own = lax.dynamic_slice_in_dim(cot, chip * ROWS, ROWS, 0)
    branch_out, conv_grad = tail(
        info, got, hidden_own, cot_own, pre_own, emb_own, w_query, w_key, w_value, w_out
    )
    keep = lax.dynamic_slice_in_dim(branch_out, core * BP, BP, 0)
    give = lax.dynamic_slice_in_dim(branch_out, (1 - core) * BP, BP, 0)
    taken = lax.ppermute(give, "seq", apart("seq", 1))
    mixed = (keep.astype(F32) + taken.astype(F32)).astype(BF)[None]

    wgrad = (wgrad_mine + wgrad_other).astype(BF)
    for bit in (1, 2, 4):
        wgrad = (wgrad.astype(F32) + lax.ppermute(wgrad, "dp", apart("dp", bit)).astype(F32)).astype(BF)
    wgrads = lax.all_gather(wgrad, "seq", axis=0, tiled=True).reshape(H, 4, HD, C)
    grad_out = wgrads[:, 0].reshape(C, C).astype(F32)
    grad_query, grad_key, grad_value = (
        wgrads[:, which].reshape(C, C).T.astype(F32) for which in (1, 2, 3)
    )

    parts = lax.all_to_all(conv_grad.reshape(H, 64, C), "seq", 0, 0, tiled=True)
    share = jnp.sum(parts.reshape(H, 64, C).astype(F32), axis=0).astype(BF)
    for bit in (1, 2, 4):
        share = (share.astype(F32) + lax.ppermute(share, "dp", apart("dp", bit)).astype(F32)).astype(BF)
    whole = lax.all_to_all(jnp.broadcast_to(share[None], (H, 64, C)), "seq", 0, 0, tiled=True)
    whole = whole.reshape(H * 64, C)[: KW * CG].reshape(KW, CG, G, CG)
    grad_conv = whole.transpose(0, 2, 3, 1).astype(F32)
    return (mixed, grad_conv, grad_query, grad_key, grad_value, grad_out)


def solution(mesh):
    in_specs = (P("dp", "seq"), P("dp"), P(), P(), P(), P(), P(), P(), P("dp", "seq", None))
    out_specs = (P("dp", "seq", None), P(), P(), P(), P(), P())
    return jax.shard_map(body, mesh=mesh, in_specs=in_specs, out_specs=out_specs, check_vma=False)
```

```python
import functools
import math

import jax
import jax.numpy as jnp
from jax import lax
from jax.experimental import pallas as pl
from jax.experimental.pallas import tpu as pltpu
from jax.sharding import PartitionSpec as P

H = 16
G = 4
KW = 5
DMAX = 16
MARGIN = 2 * DMAX
C = 768
CG = C // G
HD = C // H
BP = 128
BINS = 2048
ROWS = 256
BLOCKS = BINS // ROWS
PLANES = C // 128
PIECE = BP + HD
SCALE = HD ** (-0.5)
BF = jnp.bfloat16
F32 = jnp.float32
VMEM_LIMIT = 56 * 1024 * 1024
GELU_A = math.sqrt(2.0 / math.pi)
GELU_B = 0.044715
WINDOWS = (0, 1, 3, 4)
HALF = 512


def mm(left, right):
    return jnp.dot(left, right, preferred_element_type=F32)


def mm_nt(left, right):
    return lax.dot_general(left, right, (((1,), (1,)), ((), ())), preferred_element_type=F32)


def vmem():
    return pl.BlockSpec(memory_space=pltpu.VMEM)


def smem():
    return pl.BlockSpec(memory_space=pltpu.SMEM)


def params(**extra):
    return pltpu.CompilerParams(vmem_limit_bytes=VMEM_LIMIT, **extra)


def front_kernel(info, pieces, w_stem, conv, hidden, pre_own, emb_own, stem, emb):
    step = info[0]
    core = info[1]
    chip = info[2]
    row = lax.broadcasted_iota(jnp.int32, (4 * BP, 4 * BP), 0)
    col = lax.broadcasted_iota(jnp.int32, (4 * BP, 4 * BP), 1)
    source = 4 * (row & (BP - 1)) + (row >> 7)
    source = jnp.where(core == 1, 4 * BP - 1 - source, source)
    stem[...] = mm((col == source).astype(BF), w_stem[...]).astype(BF)
    edge = jnp.zeros((PLANES, MARGIN, 128), F32)
    emb[:, 0:MARGIN, :] = edge
    emb[:, MARGIN + BINS : MARGIN + BINS + MARGIN, :] = edge

    def embed(block, carry):
        letters = pieces[pl.ds(2 * block, 2), 0:BP, :].astype(F32).reshape(ROWS, BP)
        hot = jnp.concatenate([(letters == float(c)).astype(BF) for c in range(4)], axis=1)
        rows = mm(hot, stem[...]).astype(BF).astype(F32)
        start = pl.multiple_of(MARGIN + block * ROWS, 8)
        for plane in range(PLANES):
            emb[plane, pl.ds(start, ROWS), :] = rows[:, plane * 128 : (plane + 1) * 128]
        return carry

    lax.fori_loop(0, BLOCKS, embed, 0)

    def convolve(block, carry):
        base = MARGIN + block * ROWS
        planes = [
            [
                emb[plane, pl.ds(base + (tap - KW // 2) * step, ROWS), :].astype(BF)
                for tap in range(KW)
            ]
            for plane in range(PLANES)
        ]
        sums = []
        for group in range(G):
            at = WINDOWS[group]
            left = jnp.concatenate(
                [planes[at + half][tap] for tap in range(KW) for half in range(2)], axis=1
            )
            sums.append(mm(left, conv[group]))
        for pair in range(2):
            even, odd = sums[2 * pair], sums[2 * pair + 1]
            thirds = (even[:, :128], even[:, 128:] + odd[:, :128], odd[:, 128:])
            for third in range(3):
                plane = 3 * pair + third
                x = thirds[third]
                lanes = slice(plane * 128, (plane + 1) * 128)

                @pl.when(block == chip)
                def _(x=x, lanes=lanes):
                    pre_own[:, lanes] = x

                th = jnp.tanh(GELU_A * (x + GELU_B * (x * x * x)))
                act = 0.5 * x * (1.0 + th)
                own = emb[plane, pl.ds(pl.multiple_of(base, 8), ROWS), :]
                hidden[pl.ds(pl.multiple_of(block * ROWS, ROWS), ROWS), lanes] = (own + act).astype(BF)
        return carry

    lax.fori_loop(0, BLOCKS, convolve, 0)
    emb_own[...] = emb[:, pl.ds(pl.multiple_of(chip * ROWS, ROWS), ROWS + 2 * MARGIN), :]


def front(info, pieces, w_stem, conv):
    return pl.pallas_call(
        front_kernel,
        out_shape=(
            jax.ShapeDtypeStruct((BINS, C), BF),
            jax.ShapeDtypeStruct((ROWS, C), F32),
            jax.ShapeDtypeStruct((PLANES, ROWS + 2 * MARGIN, 128), F32),
        ),
        in_specs=[smem(), vmem(), vmem(), vmem()],
        out_specs=(vmem(), vmem(), vmem()),
        scratch_shapes=[
            pltpu.VMEM((4 * BP, C), BF),
            pltpu.VMEM((PLANES, BINS + 2 * MARGIN, 128), F32),
        ],
        compiler_params=params(),
        cost_estimate=pl.CostEstimate(flops=2 * 10**10, bytes_accessed=10**7, transcendentals=0),
        name="front",
    )(info, pieces, w_stem, conv)


def heads_kernel(
    hidden, pieces, w_qkv, out,
    q_pad, k_nat, v_nat, q_t, k_t, v_t, ga_t, x_t, scores, rounded, kv_sum,
):
    def project(block, carry):
        rows = pl.ds(pl.multiple_of(block * ROWS, ROWS), ROWS)
        y = mm(hidden[rows, :], w_qkv[...]).astype(BF)
        q_pad[rows, :] = y[:, 0:128]
        k_nat[rows, :] = y[:, 128 : 128 + HD]
        v_nat[rows, :] = y[:, 256 : 256 + HD]
        turned = y.astype(F32).T
        q_t[:, rows] = turned[0:HD].astype(BF)
        k_t[:, rows] = turned[128 : 128 + HD].astype(BF)
        v_t[:, rows] = turned[256 : 256 + HD].astype(BF)
        ga_t[:, rows] = jnp.concatenate([pieces[2 * block, BP:, :], pieces[2 * block + 1, BP:, :]], axis=1)
        return carry

    lax.fori_loop(0, BLOCKS, project, 0)
    kv_sum[...] = jnp.zeros_like(kv_sum)

    def attend(block, carry):
        lanes = pl.ds(pl.multiple_of(block * ROWS, ROWS), ROWS)
        qt = q_t[:, lanes]
        gat = ga_t[:, lanes]
        top = None
        for part in range(BLOCKS):
            at = slice(part * ROWS, (part + 1) * ROWS)
            s = mm(k_nat[at, :], qt)
            scores[at, :] = s
            most = jnp.max(s.reshape(ROWS // 8, 8, ROWS), axis=0)
            top = most if top is None else jnp.maximum(top, most)
        top = jnp.max(top, axis=0, keepdims=True)
        total = None
        for part in range(BLOCKS):
            at = slice(part * ROWS, (part + 1) * ROWS)
            e = jnp.exp2((scores[at, :] - top) * (SCALE * math.log2(math.e)))
            scores[at, :] = e
            some = jnp.sum(e.reshape(ROWS // 8, 8, ROWS), axis=0)
            total = some if total is None else total + some
        inverse = 1.0 / jnp.sum(total, axis=0, keepdims=True)
        attn = None
        for part in range(BLOCKS):
            at = slice(part * ROWS, (part + 1) * ROWS)
            pb = (scores[at, :] * inverse).astype(BF)
            rounded[at, :] = pb
            term = mm(v_t[:, at], pb)
            attn = term if attn is None else attn + term
        attn = attn.astype(BF)
        x_t[0:HD, lanes] = attn
        row_dot = jnp.sum(gat.astype(F32) * attn.astype(F32), axis=0, keepdims=True)
        ga_pad = jnp.concatenate(
            [jnp.zeros((HD, ROWS), F32), gat.astype(F32), jnp.zeros((128 - 2 * HD, ROWS), F32)], axis=0
        ).T.astype(BF)
        right = jnp.concatenate([q_pad[lanes, :], ga_pad], axis=0)
        gq = None
        for part in range(BLOCKS):
            at = slice(part * ROWS, (part + 1) * ROWS)
            gp = mm(v_nat[at, :], gat)
            gs = ((scores[at, :] * inverse) * (gp - row_dot)).astype(BF)
            term = mm(k_t[:, at], gs)
            gq = term if gq is None else gq + term
            kv_sum[at, :] += mm(jnp.concatenate([gs, rounded[at, :]], axis=1), right)
        x_t[HD : 2 * HD, lanes] = (gq * SCALE).astype(BF)
        return carry

    lax.fori_loop(0, BLOCKS, attend, 0)

    def finish(block, carry):
        rows = pl.ds(pl.multiple_of(block * ROWS, ROWS), ROWS)
        turned = kv_sum[rows, :].T
        x_t[2 * HD : 3 * HD, rows] = (turned[0:HD] * SCALE).astype(BF)
        x_t[3 * HD : 4 * HD, rows] = turned[HD : 2 * HD].astype(BF)
        out[block] = x_t[:, rows]
        return carry

    lax.fori_loop(0, BLOCKS, finish, 0)


def heads(hidden, pieces, w_qkv):
    return pl.pallas_call(
        heads_kernel,
        out_shape=jax.ShapeDtypeStruct((BLOCKS, 4 * HD, ROWS), BF),
        in_specs=[vmem()] * 3,
        out_specs=vmem(),
        scratch_shapes=[
            pltpu.VMEM((BINS, 128), BF),
            pltpu.VMEM((BINS, HD), BF),
            pltpu.VMEM((BINS, HD), BF),
            pltpu.VMEM((HD, BINS), BF),
            pltpu.VMEM((HD, BINS), BF),
            pltpu.VMEM((HD, BINS), BF),
            pltpu.VMEM((HD, BINS), BF),
            pltpu.VMEM((4 * HD, BINS), BF),
            pltpu.VMEM((BINS, ROWS), F32),
            pltpu.VMEM((BINS, ROWS), BF),
            pltpu.VMEM((BINS, 128), F32),
        ],
        compiler_params=params(),
        cost_estimate=pl.CostEstimate(flops=4 * 10**10, bytes_accessed=10**7, transcendentals=0),
        name="heads",
    )(hidden, pieces, w_qkv)


def weights_kernel(mine, other, hidden_mine, hidden_other, cot, out, from_cot, from_hidden):
    from_cot[...] = jnp.zeros_like(from_cot)
    from_hidden[...] = jnp.zeros_like(from_hidden)

    def add(block, carry):
        rows = pl.ds(pl.multiple_of(block * ROWS, ROWS), ROWS)
        one, two = mine[block], other[block]
        from_cot[...] += mm(jnp.concatenate([one[:HD], two[:HD]], axis=0), cot[rows, :])
        from_hidden[...] += mm(one[HD:], hidden_mine[rows, :]) + mm(two[HD:], hidden_other[rows, :])
        return carry

    lax.fori_loop(0, BLOCKS, add, 0)
    out[0:HD, :] = (from_cot[0:HD, :] + from_cot[HD:, :]).astype(BF)
    out[HD:, :] = from_hidden[...].astype(BF)


def weights(mine, other, hidden_mine, hidden_other, cot):
    return pl.pallas_call(
        weights_kernel,
        out_shape=jax.ShapeDtypeStruct((4 * HD, C), BF),
        in_specs=[vmem()] * 5,
        out_specs=vmem(),
        scratch_shapes=[pltpu.VMEM((2 * HD, C), F32), pltpu.VMEM((3 * HD, C), F32)],
        compiler_params=params(),
        cost_estimate=pl.CostEstimate(flops=2 * 10**9, bytes_accessed=10**7, transcendentals=0),
        name="weights",
    )(mine, other, hidden_mine, hidden_other, cot)


def tail_kernel(
    info, got_same, got_cross, hidden, cot, pre, emb, w_query, w_key, w_value, w_out,
    out_keep, out_give, conv_keep, conv_give, branch_out, conv_grad,
):
    step = info[0]
    core = info[1]
    same, cross = got_same[...], got_cross[...]
    even = jnp.where(core == 0, same, cross)
    odd = jnp.where(core == 0, cross, same)

    def rows_of(which):
        at = slice(which * HD, (which + 1) * HD)
        part = jnp.concatenate([x[chip, at] for chip in range(H // 2) for x in (even, odd)], axis=0)
        return part.astype(F32).T.astype(BF)

    branch_out[...] = hidden[...].astype(F32) + mm(rows_of(0), w_out[...])
    out_keep[...] = branch_out[pl.ds(pl.multiple_of(core * BP, BP), BP), :].astype(BF)
    out_give[...] = branch_out[pl.ds(pl.multiple_of((1 - core) * BP, BP), BP), :].astype(BF)
    grad = cot[...].astype(F32) + mm_nt(rows_of(1), w_query[...])
    grad = grad + mm_nt(rows_of(2), w_key[...])
    grad = grad + mm_nt(rows_of(3), w_value[...])
    x = pre[...]
    square = x * x
    th = jnp.tanh(GELU_A * (x + GELU_B * (square * x)))
    slope = 0.5 * (1.0 + th) + 0.5 * x * (1.0 - th * th) * (GELU_A * (1.0 + 3.0 * GELU_B * square))
    grad_t = (grad * slope).astype(BF).astype(F32).T.astype(BF)
    low = lax.broadcasted_iota(jnp.int32, (CG, 128), 1) < 64
    for tap in range(KW):
        start = MARGIN + (tap - KW // 2) * step
        planes = [emb[plane, pl.ds(start, ROWS), :].astype(BF) for plane in range(PLANES)]
        for pair in range(2):
            terms = []
            for half in range(2):
                group = 2 * pair + half
                at = WINDOWS[group]
                right = jnp.concatenate([planes[at], planes[at + 1]], axis=1)
                terms.append(mm(grad_t[group * CG : (group + 1) * CG], right))
            first, last = terms
            thirds = (first[:, :128], jnp.where(low, first[:, 128:], last[:, :128]), last[:, 128:])
            for third in range(3):
                plane = 3 * pair + third
                conv_grad[tap * CG : (tap + 1) * CG, plane * 128 : (plane + 1) * 128] = thirds[third]
    conv_grad[KW * CG :, :] = jnp.zeros((HALF * 2 - KW * CG, C), F32)
    conv_keep[...] = conv_grad[pl.ds(pl.multiple_of(core * HALF, HALF), HALF), :].astype(BF)
    conv_give[...] = conv_grad[pl.ds(pl.multiple_of((1 - core) * HALF, HALF), HALF), :].astype(BF)


def tail(info, got_same, got_cross, hidden, cot, pre, emb, w_query, w_key, w_value, w_out):
    def whole(x):
        return pl.BlockSpec(x.shape, lambda i, info: (0,) * x.ndim)

    own = pl.BlockSpec((ROWS, C), lambda i, info: (info[2], 0))
    outs = [jax.ShapeDtypeStruct(s, BF) for s in ((BP, C), (BP, C), (HALF, C), (HALF, C))]
    return pl.pallas_call(
        tail_kernel,
        out_shape=outs,
        grid_spec=pltpu.PrefetchScalarGridSpec(
            num_scalar_prefetch=1,
            grid=(1,),
            in_specs=[whole(got_same), whole(got_cross), own, own]
            + [whole(x) for x in (pre, emb, w_query, w_key, w_value, w_out)],
            out_specs=[whole(x) for x in outs],
            scratch_shapes=[pltpu.VMEM((ROWS, C), F32), pltpu.VMEM((2 * HALF, C), F32)],
        ),
        compiler_params=params(),
        cost_estimate=pl.CostEstimate(flops=5 * 10**9, bytes_accessed=10**7, transcendentals=0),
        name="tail",
    )(info, got_same, got_cross, hidden, cot, pre, emb, w_query, w_key, w_value, w_out)


def unpack_weights_kernel(parts, *outs):
    for which in range(4):
        part = parts[:, which * HD : (which + 1) * HD, :].reshape(C, C).astype(F32)
        outs[which][...] = part if which == 0 else part.T


def unpack_weights(parts):
    return pl.pallas_call(
        unpack_weights_kernel,
        out_shape=[jax.ShapeDtypeStruct((C, C), F32)] * 4,
        in_specs=[vmem()],
        out_specs=[vmem()] * 4,
        compiler_params=params(),
        cost_estimate=pl.CostEstimate(flops=10**7, bytes_accessed=14 * 10**6, transcendentals=0),
        name="unpack_weights",
    )(parts)


def unpack_conv_kernel(info, mine, other, out):
    core = info[1]
    mine, other = mine[...], other[...]
    low = jnp.where(core == 0, mine, other)
    high = jnp.where(core == 0, other, mine)
    full = jnp.concatenate([low, high], axis=0)
    for tap in range(KW):
        out[tap] = full[tap * CG : (tap + 1) * CG].astype(F32).T.reshape(G, CG, CG)


def unpack_conv(info, mine, other):
    return pl.pallas_call(
        unpack_conv_kernel,
        out_shape=jax.ShapeDtypeStruct((KW, G, CG, CG), F32),
        in_specs=[smem(), vmem(), vmem()],
        out_specs=vmem(),
        compiler_params=params(),
        cost_estimate=pl.CostEstimate(flops=10**7, bytes_accessed=5 * 10**6, transcendentals=0),
        name="unpack_conv",
    )(info, mine, other)


SWAP = [(0, 1), (1, 0)]
SEQ = ("chip", "core")
ALL_CHIPS = ("dp", "chip")


def to_chips(x, axes):
    return lax.all_to_all(x, axes, 0, 0, tiled=True)


def body(tokens, dilation, w_stem, conv_w, w_query, w_key, w_value, w_out, cotangent):
    core = lax.axis_index("core")
    chip = lax.axis_index("chip")
    me = lax.axis_index(SEQ)
    step = jnp.where(core == 1, -dilation[0], dilation[0])
    info = jnp.stack([step, core, chip]).astype(jnp.int32)
    own_cot = cotangent[0]
    ga_t = lax.dot_general(w_out, own_cot, (((1,), (1,)), ((), ())), preferred_element_type=F32).astype(BF)
    letters = jnp.broadcast_to(tokens.reshape(1, BP, BP).astype(BF), (H, BP, BP))
    pieces = to_chips(jnp.concatenate([letters, ga_t.reshape(H, HD, BP)], axis=1), SEQ)
    pieces, own_cot = lax.optimization_barrier((pieces, own_cot))
    cot = lax.all_gather(own_cot, SEQ, axis=0, tiled=True)
    taps = conv_w.transpose(1, 0, 2, 3)
    conv = jnp.stack(
        [
            jnp.pad(taps[group], ((0, 0), (64, 0), (64, 0)) if group % 2 else ((0, 0), (0, 64), (0, 64)))
            for group in range(G)
        ]
    ).reshape(G, KW * 256, 256)
    w_qkv = jnp.concatenate(
        [
            jnp.pad(lax.dynamic_slice_in_dim(w, me * HD, HD, 1), ((0, 0), (0, 128 - HD)))
            for w in (w_query, w_key, w_value)
        ],
        axis=1,
    )
    hidden, pre_own, emb_own = front(info, pieces, w_stem, conv)
    hidden_other = lax.ppermute(hidden, "core", SWAP)
    mine = heads(hidden, pieces, w_qkv)
    got_same = to_chips(mine, "chip")
    other = heads(hidden_other, pieces, w_qkv)
    got_cross = to_chips(lax.ppermute(other, "core", SWAP), "chip")

    wgrad = weights(mine, other, hidden, hidden_other, cot)
    wgrad = to_chips(wgrad, "dp").reshape(8, 24, C)
    wgrad = jnp.sum(wgrad.astype(F32), axis=0).astype(BF)
    wgrad = to_chips(jnp.broadcast_to(wgrad[None], (8, 24, C)), "dp").reshape(4 * HD, C)
    grad_out, grad_query, grad_key, grad_value = unpack_weights(lax.all_gather(wgrad, SEQ, axis=0))

    out_keep, out_give, conv_keep, conv_give = tail(
        info, got_same, got_cross, hidden, cot, pre_own, emb_own, w_query, w_key, w_value, w_out
    )
    conv_taken = lax.ppermute(conv_give, "core", SWAP)
    share = (conv_keep.astype(F32) + conv_taken.astype(F32)).astype(BF)
    parts = to_chips(share, ALL_CHIPS).reshape(64, HALF // 64, C)
    share = jnp.sum(parts.astype(F32), axis=0).astype(BF)
    conv_mine = to_chips(jnp.broadcast_to(share[None], (64, HALF // 64, C)), ALL_CHIPS).reshape(HALF, C)
    grad_conv = unpack_conv(info, conv_mine, lax.ppermute(conv_mine, "core", SWAP))

    taken = lax.ppermute(out_give, "core", SWAP)
    mixed = (out_keep.astype(F32) + taken.astype(F32)).astype(BF)[None]
    return (mixed, grad_conv, grad_query, grad_key, grad_value, grad_out)


def solution(mesh):
    split = jax.sharding.Mesh(mesh.devices.reshape(8, 8, 2), ("dp", "chip", "core"))
    in_specs = (P("dp", SEQ), P("dp"), P(), P(), P(), P(), P(), P(), P("dp", SEQ, None))
    out_specs = (P("dp", SEQ, None), P(), P(), P(), P(), P())
    return jax.shard_map(body, mesh=split, in_specs=in_specs, out_specs=out_specs, check_vma=False)
```

```python
import functools
import math

import jax
import jax.numpy as jnp
from jax import lax
from jax.experimental import pallas as pl
from jax.experimental.pallas import tpu as pltpu
from jax.sharding import PartitionSpec as P

H = 16
G = 4
KW = 5
DMAX = 16
MARGIN = 2 * DMAX
C = 768
CG = C // G
HD = C // H
BP = 128
BINS = 2048
ROWS = 256
BLOCKS = BINS // ROWS
PLANES = C // 128
PIECE = BP + HD
SCALE = HD ** (-0.5)
BF = jnp.bfloat16
F32 = jnp.float32
VMEM_LIMIT = 56 * 1024 * 1024
GELU_A = math.sqrt(2.0 / math.pi)
GELU_B = 0.044715
WINDOWS = (0, 1, 3, 4)
HALF = 512


def mm(left, right):
    return jnp.dot(left, right, preferred_element_type=F32)


def mm_nt(left, right):
    return lax.dot_general(left, right, (((1,), (1,)), ((), ())), preferred_element_type=F32)


def vmem():
    return pl.BlockSpec(memory_space=pltpu.VMEM)


def smem():
    return pl.BlockSpec(memory_space=pltpu.SMEM)


def params(**extra):
    return pltpu.CompilerParams(vmem_limit_bytes=VMEM_LIMIT, **extra)


def front_kernel(info, pieces, w_stem, conv, hidden, pre_own, emb_own, stem, emb):
    step = info[0]
    core = info[1]
    chip = info[2]
    row = lax.broadcasted_iota(jnp.int32, (4 * BP, 4 * BP), 0)
    col = lax.broadcasted_iota(jnp.int32, (4 * BP, 4 * BP), 1)
    source = 4 * (row & (BP - 1)) + (row >> 7)
    source = jnp.where(core == 1, 4 * BP - 1 - source, source)
    stem[...] = mm((col == source).astype(BF), w_stem[...]).astype(BF)
    edge = jnp.zeros((PLANES, MARGIN, 128), F32)
    emb[:, 0:MARGIN, :] = edge
    emb[:, MARGIN + BINS : MARGIN + BINS + MARGIN, :] = edge

    def embed(block, carry):
        letters = pieces[pl.ds(2 * block, 2), 0:BP, :].astype(F32).reshape(ROWS, BP)
        hot = jnp.concatenate([(letters == float(c)).astype(BF) for c in range(4)], axis=1)
        rows = mm(hot, stem[...]).astype(BF).astype(F32)
        start = pl.multiple_of(MARGIN + block * ROWS, 8)
        for plane in range(PLANES):
            emb[plane, pl.ds(start, ROWS), :] = rows[:, plane * 128 : (plane + 1) * 128]
        return carry

    lax.fori_loop(0, BLOCKS, embed, 0)

    def convolve(block, carry):
        base = MARGIN + block * ROWS
        planes = [
            [
                emb[plane, pl.ds(base + (tap - KW // 2) * step, ROWS), :].astype(BF)
                for tap in range(KW)
            ]
            for plane in range(PLANES)
        ]
        sums = []
        for group in range(G):
            at = WINDOWS[group]
            left = jnp.concatenate(
                [planes[at + half][tap] for tap in range(KW) for half in range(2)], axis=1
            )
            sums.append(mm(left, conv[group]))
        for pair in range(2):
            even, odd = sums[2 * pair], sums[2 * pair + 1]
            thirds = (even[:, :128], even[:, 128:] + odd[:, :128], odd[:, 128:])
            for third in range(3):
                plane = 3 * pair + third
                x = thirds[third]
                lanes = slice(plane * 128, (plane + 1) * 128)

                @pl.when(block == chip)
                def _(x=x, lanes=lanes):
                    pre_own[:, lanes] = x

                th = jnp.tanh(GELU_A * (x + GELU_B * (x * x * x)))
                act = 0.5 * x * (1.0 + th)
                own = emb[plane, pl.ds(pl.multiple_of(base, 8), ROWS), :]
                hidden[pl.ds(pl.multiple_of(block * ROWS, ROWS), ROWS), lanes] = (own + act).astype(BF)
        return carry

    lax.fori_loop(0, BLOCKS, convolve, 0)
    emb_own[...] = emb[:, pl.ds(pl.multiple_of(chip * ROWS, ROWS), ROWS + 2 * MARGIN), :]


def front(info, pieces, w_stem, conv):
    return pl.pallas_call(
        front_kernel,
        out_shape=(
            jax.ShapeDtypeStruct((BINS, C), BF),
            jax.ShapeDtypeStruct((ROWS, C), F32),
            jax.ShapeDtypeStruct((PLANES, ROWS + 2 * MARGIN, 128), F32),
        ),
        in_specs=[smem(), vmem(), vmem(), vmem()],
        out_specs=(vmem(), vmem(), vmem()),
        scratch_shapes=[
            pltpu.VMEM((4 * BP, C), BF),
            pltpu.VMEM((PLANES, BINS + 2 * MARGIN, 128), F32),
        ],
        compiler_params=params(),
        cost_estimate=pl.CostEstimate(flops=2 * 10**10, bytes_accessed=10**7, transcendentals=0),
        name="front",
    )(info, pieces, w_stem, conv)


def heads_kernel(
    hidden, pieces, w_qkv, out,
    q_pad, k_nat, v_nat, q_t, k_t, v_t, ga_t, x_t, scores, rounded, kv_sum,
):
    def project(block, carry):
        rows = pl.ds(pl.multiple_of(block * ROWS, ROWS), ROWS)
        y = mm(hidden[rows, :], w_qkv[...]).astype(BF)
        q_pad[rows, :] = y[:, 0:128]
        k_nat[rows, :] = y[:, 128 : 128 + HD]
        v_nat[rows, :] = y[:, 256 : 256 + HD]
        turned = y.astype(F32).T
        q_t[:, rows] = turned[0:HD].astype(BF)
        k_t[:, rows] = turned[128 : 128 + HD].astype(BF)
        v_t[:, rows] = turned[256 : 256 + HD].astype(BF)
        ga_t[:, rows] = jnp.concatenate([pieces[2 * block, BP:, :], pieces[2 * block + 1, BP:, :]], axis=1)
        return carry

    lax.fori_loop(0, BLOCKS, project, 0)
    kv_sum[...] = jnp.zeros_like(kv_sum)

    def attend(block, carry):
        lanes = pl.ds(pl.multiple_of(block * ROWS, ROWS), ROWS)
        qt = q_t[:, lanes]
        gat = ga_t[:, lanes]
        top = None
        for part in range(BLOCKS):
            at = slice(part * ROWS, (part + 1) * ROWS)
            s = mm(k_nat[at, :], qt)
            scores[at, :] = s
            most = jnp.max(s.reshape(ROWS // 8, 8, ROWS), axis=0)
            top = most if top is None else jnp.maximum(top, most)
        top = jnp.max(top, axis=0, keepdims=True)
        total = None
        for part in range(BLOCKS):
            at = slice(part * ROWS, (part + 1) * ROWS)
            e = jnp.exp2((scores[at, :] - top) * (SCALE * math.log2(math.e)))
            scores[at, :] = e
            some = jnp.sum(e.reshape(ROWS // 8, 8, ROWS), axis=0)
            total = some if total is None else total + some
        inverse = 1.0 / jnp.sum(total, axis=0, keepdims=True)
        attn = None
        for part in range(BLOCKS):
            at = slice(part * ROWS, (part + 1) * ROWS)
            pb = (scores[at, :] * inverse).astype(BF)
            rounded[at, :] = pb
            term = mm(v_t[:, at], pb)
            attn = term if attn is None else attn + term
        attn = attn.astype(BF)
        x_t[0:HD, lanes] = attn
        row_dot = jnp.sum(gat.astype(F32) * attn.astype(F32), axis=0, keepdims=True)
        ga_pad = jnp.concatenate(
            [jnp.zeros((HD, ROWS), F32), gat.astype(F32), jnp.zeros((128 - 2 * HD, ROWS), F32)], axis=0
        ).T.astype(BF)
        right = jnp.concatenate([q_pad[lanes, :], ga_pad], axis=0)
        gq = None
        for part in range(BLOCKS):
            at = slice(part * ROWS, (part + 1) * ROWS)
            gp = mm(v_nat[at, :], gat)
            gs = ((scores[at, :] * inverse) * (gp - row_dot)).astype(BF)
            term = mm(k_t[:, at], gs)
            gq = term if gq is None else gq + term
            kv_sum[at, :] += mm(jnp.concatenate([gs, rounded[at, :]], axis=1), right)
        x_t[HD : 2 * HD, lanes] = (gq * SCALE).astype(BF)
        return carry

    lax.fori_loop(0, BLOCKS, attend, 0)

    def finish(block, carry):
        rows = pl.ds(pl.multiple_of(block * ROWS, ROWS), ROWS)
        turned = kv_sum[rows, :].T
        x_t[2 * HD : 3 * HD, rows] = (turned[0:HD] * SCALE).astype(BF)
        x_t[3 * HD : 4 * HD, rows] = turned[HD : 2 * HD].astype(BF)
        out[block] = x_t[:, rows]
        return carry

    lax.fori_loop(0, BLOCKS, finish, 0)


def heads(hidden, pieces, w_qkv):
    return pl.pallas_call(
        heads_kernel,
        out_shape=jax.ShapeDtypeStruct((BLOCKS, 4 * HD, ROWS), BF),
        in_specs=[vmem()] * 3,
        out_specs=vmem(),
        scratch_shapes=[
            pltpu.VMEM((BINS, 128), BF),
            pltpu.VMEM((BINS, HD), BF),
            pltpu.VMEM((BINS, HD), BF),
            pltpu.VMEM((HD, BINS), BF),
            pltpu.VMEM((HD, BINS), BF),
            pltpu.VMEM((HD, BINS), BF),
            pltpu.VMEM((HD, BINS), BF),
            pltpu.VMEM((4 * HD, BINS), BF),
            pltpu.VMEM((BINS, ROWS), F32),
            pltpu.VMEM((BINS, ROWS), BF),
            pltpu.VMEM((BINS, 128), F32),
        ],
        compiler_params=params(),
        cost_estimate=pl.CostEstimate(flops=4 * 10**10, bytes_accessed=10**7, transcendentals=0),
        name="heads",
    )(hidden, pieces, w_qkv)


def weights_kernel(mine, other, hidden_mine, hidden_other, cot, out, from_cot, from_hidden):
    @pl.when(pl.program_id(0) == 0)
    def _():
        from_cot[...] = jnp.zeros_like(from_cot)
        from_hidden[...] = jnp.zeros_like(from_hidden)

    one, two = mine[0], other[0]
    from_cot[...] += mm(one[:HD], cot[...]) + mm(two[:HD], cot[...])
    from_hidden[...] += mm(one[HD:], hidden_mine[...]) + mm(two[HD:], hidden_other[...])

    @pl.when(pl.program_id(0) == BLOCKS - 1)
    def _():
        out[0:HD, :] = from_cot[...].astype(BF)
        out[HD:, :] = from_hidden[...].astype(BF)


def weights(mine, other, hidden_mine, hidden_other, cot):
    piece = pl.BlockSpec((1, 4 * HD, ROWS), lambda i: (i, 0, 0))
    rows = pl.BlockSpec((ROWS, C), lambda i: (i, 0))
    return pl.pallas_call(
        weights_kernel,
        out_shape=jax.ShapeDtypeStruct((4 * HD, C), BF),
        grid=(BLOCKS,),
        in_specs=[piece, piece, rows, rows, rows],
        out_specs=pl.BlockSpec((4 * HD, C), lambda i: (0, 0)),
        scratch_shapes=[pltpu.VMEM((HD, C), F32), pltpu.VMEM((3 * HD, C), F32)],
        compiler_params=params(),
        cost_estimate=pl.CostEstimate(flops=2 * 10**9, bytes_accessed=10**7, transcendentals=0),
        name="weights",
    )(mine, other, hidden_mine, hidden_other, cot)


def tail_kernel(
    info, got_same, got_cross, hidden, cot, pre, emb, w_query, w_key, w_value, w_out,
    out_keep, out_give, conv_keep, conv_give, branch_out, conv_grad,
):
    step = info[0]
    core = info[1]
    same, cross = got_same[...], got_cross[...]
    even = jnp.where(core == 0, same, cross)
    odd = jnp.where(core == 0, cross, same)

    def rows_of(which):
        at = slice(which * HD, (which + 1) * HD)
        part = jnp.concatenate([x[chip, at] for chip in range(H // 2) for x in (even, odd)], axis=0)
        return part.astype(F32).T.astype(BF)

    branch_out[...] = hidden[...].astype(F32) + mm(rows_of(0), w_out[...])
    out_keep[...] = branch_out[pl.ds(pl.multiple_of(core * BP, BP), BP), :].astype(BF)
    out_give[...] = branch_out[pl.ds(pl.multiple_of((1 - core) * BP, BP), BP), :].astype(BF)
    grad = cot[...].astype(F32) + mm_nt(rows_of(1), w_query[...])
    grad = grad + mm_nt(rows_of(2), w_key[...])
    grad = grad + mm_nt(rows_of(3), w_value[...])
    x = pre[...]
    square = x * x
    th = jnp.tanh(GELU_A * (x + GELU_B * (square * x)))
    slope = 0.5 * (1.0 + th) + 0.5 * x * (1.0 - th * th) * (GELU_A * (1.0 + 3.0 * GELU_B * square))
    grad_t = (grad * slope).astype(BF).astype(F32).T.astype(BF)
    low = lax.broadcasted_iota(jnp.int32, (CG, 128), 1) < 64
    for tap in range(KW):
        start = MARGIN + (tap - KW // 2) * step
        planes = [emb[plane, pl.ds(start, ROWS), :].astype(BF) for plane in range(PLANES)]
        for pair in range(2):
            terms = []
            for half in range(2):
                group = 2 * pair + half
                at = WINDOWS[group]
                right = jnp.concatenate([planes[at], planes[at + 1]], axis=1)
                terms.append(mm(grad_t[group * CG : (group + 1) * CG], right))
            first, last = terms
            thirds = (first[:, :128], jnp.where(low, first[:, 128:], last[:, :128]), last[:, 128:])
            for third in range(3):
                plane = 3 * pair + third
                conv_grad[tap * CG : (tap + 1) * CG, plane * 128 : (plane + 1) * 128] = thirds[third]
    conv_grad[KW * CG :, :] = jnp.zeros((HALF * 2 - KW * CG, C), F32)
    conv_keep[...] = conv_grad[pl.ds(pl.multiple_of(core * HALF, HALF), HALF), :].astype(BF)
    conv_give[...] = conv_grad[pl.ds(pl.multiple_of((1 - core) * HALF, HALF), HALF), :].astype(BF)


def tail(info, got_same, got_cross, hidden, cot, pre, emb, w_query, w_key, w_value, w_out):
    def whole(x):
        return pl.BlockSpec(x.shape, lambda i, info: (0,) * x.ndim)

    own = pl.BlockSpec((ROWS, C), lambda i, info: (info[2], 0))
    outs = [jax.ShapeDtypeStruct(s, BF) for s in ((BP, C), (BP, C), (HALF, C), (HALF, C))]
    return pl.pallas_call(
        tail_kernel,
        out_shape=outs,
        grid_spec=pltpu.PrefetchScalarGridSpec(
            num_scalar_prefetch=1,
            grid=(1,),
            in_specs=[whole(got_same), whole(got_cross), own, own]
            + [whole(x) for x in (pre, emb, w_query, w_key, w_value, w_out)],
            out_specs=[whole(x) for x in outs],
            scratch_shapes=[pltpu.VMEM((ROWS, C), F32), pltpu.VMEM((2 * HALF, C), F32)],
        ),
        compiler_params=params(),
        cost_estimate=pl.CostEstimate(flops=5 * 10**9, bytes_accessed=10**7, transcendentals=0),
        name="tail",
    )(info, got_same, got_cross, hidden, cot, pre, emb, w_query, w_key, w_value, w_out)


def unpack_weights_kernel(parts, *outs):
    for which in range(4):
        part = parts[:, which * HD : (which + 1) * HD, :].reshape(C, C).astype(F32)
        outs[which][...] = part if which == 0 else part.T


def unpack_weights(parts):
    return pl.pallas_call(
        unpack_weights_kernel,
        out_shape=[jax.ShapeDtypeStruct((C, C), F32)] * 4,
        in_specs=[vmem()],
        out_specs=[vmem()] * 4,
        compiler_params=params(),
        cost_estimate=pl.CostEstimate(flops=10**7, bytes_accessed=14 * 10**6, transcendentals=0),
        name="unpack_weights",
    )(parts)


def unpack_conv_kernel(info, mine, other, out):
    core = info[1]
    mine, other = mine[...], other[...]
    low = jnp.where(core == 0, mine, other)
    high = jnp.where(core == 0, other, mine)
    full = jnp.concatenate([low, high], axis=0)
    for tap in range(KW):
        out[tap] = full[tap * CG : (tap + 1) * CG].astype(F32).T.reshape(G, CG, CG)


def unpack_conv(info, mine, other):
    return pl.pallas_call(
        unpack_conv_kernel,
        out_shape=jax.ShapeDtypeStruct((KW, G, CG, CG), F32),
        in_specs=[smem(), vmem(), vmem()],
        out_specs=vmem(),
        compiler_params=params(),
        cost_estimate=pl.CostEstimate(flops=10**7, bytes_accessed=5 * 10**6, transcendentals=0),
        name="unpack_conv",
    )(info, mine, other)


SWAP = [(0, 1), (1, 0)]
SEQ = ("chip", "core")
ALL_CHIPS = ("dp", "chip")


def apart(axis, bit):
    return [(i, i ^ bit) for i in range(lax.axis_size(axis))]


def to_chips(x, axes):
    return lax.all_to_all(x, axes, 0, 0, tiled=True)


def body(tokens, dilation, w_stem, conv_w, w_query, w_key, w_value, w_out, cotangent):
    core = lax.axis_index("core")
    chip = lax.axis_index("chip")
    me = lax.axis_index(SEQ)
    step = jnp.where(core == 1, -dilation[0], dilation[0])
    info = jnp.stack([step, core, chip]).astype(jnp.int32)
    own_cot = cotangent[0]
    ga_t = lax.dot_general(w_out, own_cot, (((1,), (1,)), ((), ())), preferred_element_type=F32).astype(BF)
    letters = jnp.broadcast_to(tokens.reshape(1, BP, BP).astype(BF), (H, BP, BP))
    pieces = to_chips(jnp.concatenate([letters, ga_t.reshape(H, HD, BP)], axis=1), SEQ)
    pieces, own_cot = lax.optimization_barrier((pieces, own_cot))
    cot = lax.all_gather(own_cot, SEQ, axis=0, tiled=True)
    taps = conv_w.transpose(1, 0, 2, 3)
    conv = jnp.stack(
        [
            jnp.pad(taps[group], ((0, 0), (64, 0), (64, 0)) if group % 2 else ((0, 0), (0, 64), (0, 64)))
            for group in range(G)
        ]
    ).reshape(G, KW * 256, 256)
    w_qkv = jnp.concatenate(
        [
            jnp.pad(lax.dynamic_slice_in_dim(w, me * HD, HD, 1), ((0, 0), (0, 128 - HD)))
            for w in (w_query, w_key, w_value)
        ],
        axis=1,
    )
    hidden, pre_own, emb_own = front(info, pieces, w_stem, conv)
    hidden_other = lax.ppermute(hidden, "core", SWAP)
    mine = heads(hidden, pieces, w_qkv)
    got_same = to_chips(mine, "chip")
    other = heads(hidden_other, pieces, w_qkv)
    mine, other, got_same = lax.optimization_barrier((mine, other, got_same))
    got_cross = to_chips(lax.ppermute(other, "core", SWAP), "chip")
    wgrad = weights(mine, other, hidden, hidden_other, cot)
    once = lax.ppermute(wgrad, "dp", apart("dp", 1))
    once, got_cross = lax.optimization_barrier((once, got_cross))
    wgrad = (wgrad.astype(F32) + once.astype(F32)).astype(BF)
    twice = lax.ppermute(wgrad, "dp", apart("dp", 2))
    out_keep, out_give, conv_keep, conv_give = tail(
        info, got_same, got_cross, hidden, cot, pre_own, emb_own, w_query, w_key, w_value, w_out
    )
    twice, conv_give, out_give = lax.optimization_barrier((twice, conv_give, out_give))
    wgrad = (wgrad.astype(F32) + twice.astype(F32)).astype(BF)
    thrice = lax.ppermute(wgrad, "dp", apart("dp", 4))
    conv_taken = lax.ppermute(conv_give, "core", SWAP)
    share = (conv_keep.astype(F32) + conv_taken.astype(F32)).astype(BF)
    parts = to_chips(share, ALL_CHIPS).reshape(64, HALF // 64, C)
    thrice, parts = lax.optimization_barrier((thrice, parts))
    wgrad = (wgrad.astype(F32) + thrice.astype(F32)).astype(BF)
    wgrads = lax.all_gather(wgrad, SEQ, axis=0)
    share = jnp.sum(parts.astype(F32), axis=0).astype(BF)
    conv_mine = to_chips(jnp.broadcast_to(share[None], (64, HALF // 64, C)), ALL_CHIPS).reshape(HALF, C)
    grad_conv = unpack_conv(info, conv_mine, lax.ppermute(conv_mine, "core", SWAP))

    grad_out, grad_query, grad_key, grad_value = unpack_weights(wgrads)
    taken = lax.ppermute(out_give, "core", SWAP)
    mixed = (out_keep.astype(F32) + taken.astype(F32)).astype(BF)[None]
    return (mixed, grad_conv, grad_query, grad_key, grad_value, grad_out)


def solution(mesh):
    split = jax.sharding.Mesh(mesh.devices.reshape(8, 8, 2), ("dp", "chip", "core"))
    in_specs = (P("dp", SEQ), P("dp"), P(), P(), P(), P(), P(), P(), P("dp", SEQ, None))
    out_specs = (P("dp", SEQ, None), P(), P(), P(), P(), P())
    return jax.shard_map(body, mesh=split, in_specs=in_specs, out_specs=out_specs, check_vma=False)
```

```python
import functools
import math

import jax
import jax.numpy as jnp
from jax import lax
from jax.experimental import pallas as pl
from jax.experimental.pallas import tpu as pltpu
from jax.sharding import PartitionSpec as P

H = 16
G = 4
KW = 5
DMAX = 16
MARGIN = 2 * DMAX
C = 768
CG = C // G
HD = C // H
BP = 128
BINS = 2048
ROWS = 256
BLOCKS = BINS // ROWS
WIDE = 1024
PLANES = C // 128
PIECE = BP + HD
SCALE = HD ** (-0.5)
BF = jnp.bfloat16
F32 = jnp.float32
VMEM_LIMIT = 56 * 1024 * 1024
GELU_A = math.sqrt(2.0 / math.pi)
GELU_B = 0.044715
WINDOWS = (0, 1, 3, 4)
HALF = 512


def mm(left, right):
    return jnp.dot(left, right, preferred_element_type=F32)


def mm_nt(left, right):
    return lax.dot_general(left, right, (((1,), (1,)), ((), ())), preferred_element_type=F32)


def vmem():
    return pl.BlockSpec(memory_space=pltpu.VMEM)


def smem():
    return pl.BlockSpec(memory_space=pltpu.SMEM)


def params(**extra):
    return pltpu.CompilerParams(vmem_limit_bytes=VMEM_LIMIT, **extra)


def front_kernel(info, pieces, w_stem, conv, hidden, pre_own, emb_own, stem, emb, pre):
    step = info[0]
    core = info[1]
    chip = info[2]
    block = pl.program_id(0)

    @pl.when(block == 0)
    def _():
        row = lax.broadcasted_iota(jnp.int32, (4 * BP, 4 * BP), 0)
        col = lax.broadcasted_iota(jnp.int32, (4 * BP, 4 * BP), 1)
        source = 4 * (row & (BP - 1)) + (row >> 7)
        source = jnp.where(core == 1, 4 * BP - 1 - source, source)
        stem[...] = mm((col == source).astype(BF), w_stem[...]).astype(BF)
        edge = jnp.zeros((PLANES, MARGIN, 128), F32)
        emb[:, 0:MARGIN, :] = edge
        emb[:, MARGIN + BINS : MARGIN + BINS + MARGIN, :] = edge

        def embed(block, carry):
            letters = pieces[pl.ds((WIDE // BP) * block, WIDE // BP), 0:BP, :].astype(F32).reshape(WIDE, BP)
            hot = jnp.concatenate([(letters == float(c)).astype(BF) for c in range(4)], axis=1)
            rows = mm(hot, stem[...]).astype(BF).astype(F32)
            start = pl.multiple_of(MARGIN + block * WIDE, 8)
            for plane in range(PLANES):
                emb[plane, pl.ds(start, WIDE), :] = rows[:, plane * 128 : (plane + 1) * 128]
            return carry

        lax.fori_loop(0, BINS // WIDE, embed, 0)

    base = MARGIN + block * WIDE
    for pair in range(2):
        planes = [
            [
                emb[3 * pair + third, pl.ds(base + (tap - KW // 2) * step, WIDE), :].astype(BF)
                for tap in range(KW)
            ]
            for third in range(3)
        ]
        even, odd = (
            mm(
                jnp.concatenate([planes[at + half][tap] for tap in range(KW) for half in range(2)], axis=1),
                conv[2 * pair + at],
            )
            for at in range(2)
        )
        thirds = (even[:, :128], even[:, 128:] + odd[:, :128], odd[:, 128:])
        for third in range(3):
            plane = 3 * pair + third
            x = thirds[third]
            lanes = slice(plane * 128, (plane + 1) * 128)
            pre[pl.ds(pl.multiple_of(block * WIDE, WIDE), WIDE), lanes] = x
            th = jnp.tanh(GELU_A * (x + GELU_B * (x * x * x)))
            act = 0.5 * x * (1.0 + th)
            own = emb[plane, pl.ds(pl.multiple_of(base, 8), WIDE), :]
            hidden[:, lanes] = (own + act).astype(BF)

    @pl.when(block == BINS // WIDE - 1)
    def _():
        pre_own[...] = pre[pl.ds(pl.multiple_of(chip * ROWS, ROWS), ROWS), :]
        emb_own[...] = emb[:, pl.ds(pl.multiple_of(chip * ROWS, ROWS), ROWS + 2 * MARGIN), :]


def front(info, pieces, w_stem, conv):
    return pl.pallas_call(
        front_kernel,
        out_shape=(
            jax.ShapeDtypeStruct((BINS, C), BF),
            jax.ShapeDtypeStruct((ROWS, C), F32),
            jax.ShapeDtypeStruct((PLANES, ROWS + 2 * MARGIN, 128), F32),
        ),
        grid=(BINS // WIDE,),
        in_specs=[
            smem(),
            pl.BlockSpec(pieces.shape, lambda i: (0, 0, 0)),
            pl.BlockSpec(w_stem.shape, lambda i: (0, 0)),
            pl.BlockSpec(conv.shape, lambda i: (0, 0, 0)),
        ],
        out_specs=(
            pl.BlockSpec((WIDE, C), lambda i: (i, 0)),
            pl.BlockSpec((ROWS, C), lambda i: (0, 0)),
            pl.BlockSpec((PLANES, ROWS + 2 * MARGIN, 128), lambda i: (0, 0, 0)),
        ),
        scratch_shapes=[
            pltpu.VMEM((4 * BP, C), BF),
            pltpu.VMEM((PLANES, BINS + 2 * MARGIN, 128), F32),
            pltpu.VMEM((BINS, C), F32),
        ],
        compiler_params=params(),
        cost_estimate=pl.CostEstimate(flops=2 * 10**10, bytes_accessed=10**7, transcendentals=0),
        name="front",
    )(info, pieces, w_stem, conv)


def heads_kernel(
    last, hidden, pieces, w_qkv, *refs
):
    if last:
        cot, mine, from_mine, out, wgrad = refs[:5]
    else:
        out, wgrad = refs[:2]
    q_pad, k_nat, v_nat, q_t, k_t, v_t, ga_t, x_t, scores, both, kv_sum = refs[5 if last else 2 :]

    def project(block, carry):
        rows = pl.ds(pl.multiple_of(block * ROWS, ROWS), ROWS)
        y = mm(hidden[rows, :], w_qkv[...]).astype(BF)
        q_pad[rows, :] = y[:, 0:128]
        k_nat[rows, :] = y[:, 128 : 128 + HD]
        v_nat[rows, :] = y[:, 256 : 256 + HD]
        turned = y.astype(F32).T
        q_t[:, rows] = turned[0:HD].astype(BF)
        k_t[:, rows] = turned[128 : 128 + HD].astype(BF)
        v_t[:, rows] = turned[256 : 256 + HD].astype(BF)
        ga_t[:, rows] = jnp.concatenate([pieces[2 * block, BP:, :], pieces[2 * block + 1, BP:, :]], axis=1)
        return carry

    lax.fori_loop(0, BLOCKS, project, 0)
    kv_sum[...] = jnp.zeros_like(kv_sum)

    def span(block):
        return pl.ds(pl.multiple_of(block * ROWS, ROWS), ROWS)

    def products(slot, block):
        scores[slot] = mm(k_nat[...], q_t[:, span(block)])

    def softmax(slot):
        top = None
        for part in range(BLOCKS):
            at = slice(part * ROWS, (part + 1) * ROWS)
            most = jnp.max(scores[slot, at, :].reshape(ROWS // 8, 8, ROWS), axis=0)
            top = most if top is None else jnp.maximum(top, most)
        top = jnp.max(top, axis=0, keepdims=True)
        total = None
        for part in range(BLOCKS):
            at = slice(part * ROWS, (part + 1) * ROWS)
            e = jnp.exp2((scores[slot, at, :] - top) * (SCALE * math.log2(math.e)))
            scores[slot, at, :] = e
            some = jnp.sum(e.reshape(ROWS // 8, 8, ROWS), axis=0)
            total = some if total is None else total + some
        inverse = 1.0 / jnp.sum(total, axis=0, keepdims=True)
        for part in range(BLOCKS):
            at = slice(part * ROWS, (part + 1) * ROWS)
            both[slot, at, ROWS:] = (scores[slot, at, :] * inverse).astype(BF)
        return inverse

    def mix(slot, block):
        attn = mm(v_t[...], both[slot, :, ROWS:]).astype(BF)
        x_t[0:HD, span(block)] = attn
        return jnp.sum(ga_t[:, span(block)].astype(F32) * attn.astype(F32), axis=0, keepdims=True)

    def score_grads(slot, inverse, row_dot, block):
        gat = ga_t[:, span(block)]
        for part in range(BLOCKS // 2):
            at = slice(part * 2 * ROWS, (part + 1) * 2 * ROWS)
            gp = mm(v_nat[at, :], gat)
            both[slot, at, :ROWS] = ((scores[slot, at, :] * inverse) * (gp - row_dot)).astype(BF)

    def backward(slot, block):
        ga_pad = jnp.concatenate(
            [
                jnp.zeros((HD, ROWS), F32),
                ga_t[:, span(block)].astype(F32),
                jnp.zeros((128 - 2 * HD, ROWS), F32),
            ],
            axis=0,
        ).T.astype(BF)
        right = jnp.concatenate([q_pad[span(block), :], ga_pad], axis=0)
        x_t[HD : 2 * HD, span(block)] = (mm(k_t[...], both[slot, :, :ROWS]) * SCALE).astype(BF)
        kv_sum[...] += mm(both[slot], right)

    both[1] = jnp.zeros((BINS, 2 * ROWS), BF)
    products(0, 0)

    def attend(pair, carry):
        a, b = 2 * pair, 2 * pair + 1
        inv = softmax(0)
        backward(1, jnp.maximum(b - 2, 0))
        dot = mix(0, a)
        products(1, b)
        score_grads(0, inv, dot, a)
        inv = softmax(1)
        backward(0, a)
        dot = mix(1, b)
        products(0, jnp.minimum(b + 1, BLOCKS - 1))
        score_grads(1, inv, dot, b)
        return carry

    lax.fori_loop(0, BLOCKS // 2, attend, 0)
    backward(1, BLOCKS - 1)

    def finish(block, carry):
        rows = pl.ds(pl.multiple_of(block * ROWS, ROWS), ROWS)
        turned = kv_sum[rows, :].T
        x_t[2 * HD : 3 * HD, rows] = (turned[0:HD] * SCALE).astype(BF)
        x_t[3 * HD : 4 * HD, rows] = turned[HD : 2 * HD].astype(BF)
        out[block] = x_t[:, rows]
        return carry

    lax.fori_loop(0, BLOCKS, finish, 0)
    from_hidden = mm(x_t[HD:, :], hidden[...])
    if not last:
        wgrad[...] = from_hidden
        return
    wgrad[HD:, :] = (from_hidden + from_mine[...]).astype(BF)
    attn_mine = jnp.concatenate([mine[block, 0:HD, :] for block in range(BLOCKS)], axis=1)
    from_cot = mm(jnp.concatenate([x_t[0:HD, :], attn_mine], axis=0), cot[...])
    wgrad[0:HD, :] = (from_cot[0:HD] + from_cot[HD:]).astype(BF)


def heads(hidden, pieces, w_qkv, *before):
    last = bool(before)
    return pl.pallas_call(
        functools.partial(heads_kernel, last),
        out_shape=(
            jax.ShapeDtypeStruct((BLOCKS, 4 * HD, ROWS), BF),
            jax.ShapeDtypeStruct((4 * HD, C), BF) if last else jax.ShapeDtypeStruct((3 * HD, C), F32),
        ),
        in_specs=[vmem()] * (3 + len(before)),
        out_specs=(vmem(), vmem()),
        scratch_shapes=[
            pltpu.VMEM((BINS, 128), BF),
            pltpu.VMEM((BINS, HD), BF),
            pltpu.VMEM((BINS, HD), BF),
            pltpu.VMEM((HD, BINS), BF),
            pltpu.VMEM((HD, BINS), BF),
            pltpu.VMEM((HD, BINS), BF),
            pltpu.VMEM((HD, BINS), BF),
            pltpu.VMEM((4 * HD, BINS), BF),
            pltpu.VMEM((2, BINS, ROWS), F32),
            pltpu.VMEM((2, BINS, 2 * ROWS), BF),
            pltpu.VMEM((BINS, 128), F32),
        ],
        compiler_params=params(),
        cost_estimate=pl.CostEstimate(flops=3 * 10**10, bytes_accessed=10**7, transcendentals=0),
        name="heads",
    )(hidden, pieces, w_qkv, *before)


def tail_kernel(
    info, got_same, got_cross, hidden, cot, pre, emb, w_query, w_key, w_value, w_out,
    out_keep, out_give, conv_keep, conv_give, branch_out, conv_grad,
):
    step = info[0]
    core = info[1]
    same, cross = got_same[...], got_cross[...]
    even = jnp.where(core == 0, same, cross)
    odd = jnp.where(core == 0, cross, same)

    def rows_of(which):
        at = slice(which * HD, (which + 1) * HD)
        part = jnp.concatenate([x[chip, at] for chip in range(H // 2) for x in (even, odd)], axis=0)
        return part.astype(F32).T.astype(BF)

    branch_out[...] = hidden[...].astype(F32) + mm(rows_of(0), w_out[...])
    out_keep[...] = branch_out[pl.ds(pl.multiple_of(core * BP, BP), BP), :].astype(BF)
    out_give[...] = branch_out[pl.ds(pl.multiple_of((1 - core) * BP, BP), BP), :].astype(BF)
    grad = cot[...].astype(F32) + mm_nt(rows_of(1), w_query[...])
    grad = grad + mm_nt(rows_of(2), w_key[...])
    grad = grad + mm_nt(rows_of(3), w_value[...])
    x = pre[...]
    square = x * x
    th = jnp.tanh(GELU_A * (x + GELU_B * (square * x)))
    slope = 0.5 * (1.0 + th) + 0.5 * x * (1.0 - th * th) * (GELU_A * (1.0 + 3.0 * GELU_B * square))
    grad_t = (grad * slope).astype(BF).astype(F32).T.astype(BF)
    low = lax.broadcasted_iota(jnp.int32, (CG, 128), 1) < 64
    for tap in range(KW):
        start = MARGIN + (tap - KW // 2) * step
        planes = [emb[plane, pl.ds(start, ROWS), :].astype(BF) for plane in range(PLANES)]
        for pair in range(2):
            terms = []
            for half in range(2):
                group = 2 * pair + half
                at = WINDOWS[group]
                right = jnp.concatenate([planes[at], planes[at + 1]], axis=1)
                terms.append(mm(grad_t[group * CG : (group + 1) * CG], right))
            first, last = terms
            thirds = (first[:, :128], jnp.where(low, first[:, 128:], last[:, :128]), last[:, 128:])
            for third in range(3):
                plane = 3 * pair + third
                conv_grad[tap * CG : (tap + 1) * CG, plane * 128 : (plane + 1) * 128] = thirds[third]
    conv_grad[KW * CG :, :] = jnp.zeros((HALF * 2 - KW * CG, C), F32)
    conv_keep[...] = conv_grad[pl.ds(pl.multiple_of(core * HALF, HALF), HALF), :].astype(BF)
    conv_give[...] = conv_grad[pl.ds(pl.multiple_of((1 - core) * HALF, HALF), HALF), :].astype(BF)


def tail(info, got_same, got_cross, hidden, cot, pre, emb, w_query, w_key, w_value, w_out):
    def whole(x):
        return pl.BlockSpec(x.shape, lambda i, info: (0,) * x.ndim)

    own = pl.BlockSpec((ROWS, C), lambda i, info: (info[2], 0))
    outs = [jax.ShapeDtypeStruct(s, BF) for s in ((BP, C), (BP, C), (HALF, C), (HALF, C))]
    return pl.pallas_call(
        tail_kernel,
        out_shape=outs,
        grid_spec=pltpu.PrefetchScalarGridSpec(
            num_scalar_prefetch=1,
            grid=(1,),
            in_specs=[whole(got_same), whole(got_cross), own, own]
            + [whole(x) for x in (pre, emb, w_query, w_key, w_value, w_out)],
            out_specs=[whole(x) for x in outs],
            scratch_shapes=[pltpu.VMEM((ROWS, C), F32), pltpu.VMEM((2 * HALF, C), F32)],
        ),
        compiler_params=params(),
        cost_estimate=pl.CostEstimate(flops=5 * 10**9, bytes_accessed=10**7, transcendentals=0),
        name="tail",
    )(info, got_same, got_cross, hidden, cot, pre, emb, w_query, w_key, w_value, w_out)


def unpack_weights_kernel(parts, *outs):
    for which in range(4):
        part = parts[:, which * HD : (which + 1) * HD, :].reshape(C, 256).astype(F32)
        outs[which][...] = part if which == 0 else part.T


def unpack_weights(parts):
    turned = pl.BlockSpec((256, C), lambda i: (i, 0))
    return pl.pallas_call(
        unpack_weights_kernel,
        out_shape=[jax.ShapeDtypeStruct((C, C), F32)] * 4,
        grid=(C // 256,),
        in_specs=[pl.BlockSpec((H, 4 * HD, 256), lambda i: (0, 0, i))],
        out_specs=[pl.BlockSpec((C, 256), lambda i: (0, i)), turned, turned, turned],
        compiler_params=params(),
        cost_estimate=pl.CostEstimate(flops=10**7, bytes_accessed=14 * 10**6, transcendentals=0),
        name="unpack_weights",
    )(parts)


def unpack_conv_kernel(info, mine, other, out, full):
    core = info[1]
    tap = pl.program_id(0)

    @pl.when(tap == 0)
    def _():
        full[pl.ds(pl.multiple_of(core * HALF, HALF), HALF), :] = mine[...].astype(F32)
        full[pl.ds(pl.multiple_of((1 - core) * HALF, HALF), HALF), :] = other[...].astype(F32)

    rows = full[pl.ds(pl.multiple_of(tap * CG, 8), CG), :]
    out[0] = rows.T.reshape(G, CG, CG)


def unpack_conv(info, mine, other):
    half = pl.BlockSpec((HALF, C), lambda i: (0, 0))
    return pl.pallas_call(
        unpack_conv_kernel,
        out_shape=jax.ShapeDtypeStruct((KW, G, CG, CG), F32),
        grid=(KW,),
        in_specs=[smem(), half, half],
        out_specs=pl.BlockSpec((1, G, CG, CG), lambda i: (i, 0, 0, 0)),
        scratch_shapes=[pltpu.VMEM((2 * HALF, C), F32)],
        compiler_params=params(),
        cost_estimate=pl.CostEstimate(flops=10**7, bytes_accessed=5 * 10**6, transcendentals=0),
        name="unpack_conv",
    )(info, mine, other)


SWAP = [(0, 1), (1, 0)]
SEQ = ("chip", "core")
ALL_CHIPS = ("dp", "chip")


def apart(axis, bit):
    return [(i, i ^ bit) for i in range(lax.axis_size(axis))]


def to_chips(x, axes):
    return lax.all_to_all(x, axes, 0, 0, tiled=True)


def body(tokens, dilation, w_stem, conv_w, w_query, w_key, w_value, w_out, cotangent):
    core = lax.axis_index("core")
    chip = lax.axis_index("chip")
    me = lax.axis_index(SEQ)
    step = jnp.where(core == 1, -dilation[0], dilation[0])
    info = jnp.stack([step, core, chip]).astype(jnp.int32)
    own_cot = cotangent[0]
    ga_t = lax.dot_general(w_out, own_cot, (((1,), (1,)), ((), ())), preferred_element_type=F32).astype(BF)
    letters = jnp.broadcast_to(tokens.reshape(1, BP, BP).astype(BF), (H, BP, BP))
    pieces = to_chips(jnp.concatenate([letters, ga_t.reshape(H, HD, BP)], axis=1), SEQ)
    taps = conv_w.transpose(1, 0, 2, 3)
    conv = jnp.stack(
        [
            jnp.pad(taps[group], ((0, 0), (64, 0), (64, 0)) if group % 2 else ((0, 0), (0, 64), (0, 64)))
            for group in range(G)
        ]
    ).reshape(G, KW * 256, 256)
    w_qkv = jnp.concatenate(
        [
            jnp.pad(lax.dynamic_slice_in_dim(w, me * HD, HD, 1), ((0, 0), (0, 128 - HD)))
            for w in (w_query, w_key, w_value)
        ],
        axis=1,
    )
    pieces, own_cot, conv, w_qkv, info = lax.optimization_barrier((pieces, own_cot, conv, w_qkv, info))
    cot = lax.all_gather(own_cot, SEQ, axis=0, tiled=True)
    hidden, pre_own, emb_own = front(info, pieces, w_stem, conv)
    hidden_other = lax.ppermute(hidden, "core", SWAP)
    mine, from_mine = heads(hidden, pieces, w_qkv)
    got_same = to_chips(mine, "chip")
    other, wgrad = heads(hidden_other, pieces, w_qkv, cot, mine, from_mine)
    other, wgrad, got_same = lax.optimization_barrier((other, wgrad, got_same))
    got_cross = to_chips(lax.ppermute(other, "core", SWAP), "chip")
    once = lax.ppermute(wgrad, "dp", apart("dp", 1))
    wgrad = (wgrad.astype(F32) + once.astype(F32)).astype(BF)
    twice = lax.ppermute(wgrad, "dp", apart("dp", 2))
    twice, got_cross = lax.optimization_barrier((twice, got_cross))
    wgrad = (wgrad.astype(F32) + twice.astype(F32)).astype(BF)
    thrice = lax.ppermute(wgrad, "dp", apart("dp", 4))
    out_keep, out_give, conv_keep, conv_give = tail(
        info, got_same, got_cross, hidden, cot, pre_own, emb_own, w_query, w_key, w_value, w_out
    )
    thrice, conv_give, out_give = lax.optimization_barrier((thrice, conv_give, out_give))
    wgrad = (wgrad.astype(F32) + thrice.astype(F32)).astype(BF)
    wgrads = lax.all_gather(wgrad, SEQ, axis=0)
    conv_taken = lax.ppermute(conv_give, "core", SWAP)
    share = (conv_keep.astype(F32) + conv_taken.astype(F32)).astype(BF)
    parts = to_chips(share, ALL_CHIPS).reshape(64, HALF // 64, C)
    share = jnp.sum(parts.astype(F32), axis=0).astype(BF)
    conv_mine = to_chips(jnp.broadcast_to(share[None], (64, HALF // 64, C)), ALL_CHIPS).reshape(HALF, C)
    grad_conv = unpack_conv(info, conv_mine, lax.ppermute(conv_mine, "core", SWAP))

    grad_out, grad_query, grad_key, grad_value = unpack_weights(wgrads)
    taken = lax.ppermute(out_give, "core", SWAP)
    mixed = (out_keep.astype(F32) + taken.astype(F32)).astype(BF)[None]
    return (mixed, grad_conv, grad_query, grad_key, grad_value, grad_out)


def solution(mesh):
    split = jax.sharding.Mesh(mesh.devices.reshape(8, 8, 2), ("dp", "chip", "core"))
    in_specs = (P("dp", SEQ), P("dp"), P(), P(), P(), P(), P(), P(), P("dp", SEQ, None))
    out_specs = (P("dp", SEQ, None), P(), P(), P(), P(), P())
    return jax.shard_map(body, mesh=split, in_specs=in_specs, out_specs=out_specs, check_vma=False)
```

```python
import functools
import math

import jax
import jax.numpy as jnp
from jax import lax
from jax.experimental import pallas as pl
from jax.experimental.pallas import tpu as pltpu
from jax.sharding import PartitionSpec as P

H = 16
G = 4
KW = 5
DMAX = 16
MARGIN = 2 * DMAX
C = 768
CG = C // G
HD = C // H
BP = 128
BINS = 2048
ROWS = 256
BLOCKS = BINS // ROWS
WIDE = 1024
PLANES = C // 128
PIECE = BP + HD
SCALE = HD ** (-0.5)
BF = jnp.bfloat16
F32 = jnp.float32
VMEM_LIMIT = 56 * 1024 * 1024
GELU_A = math.sqrt(2.0 / math.pi)
GELU_B = 0.044715
WINDOWS = (0, 1, 3, 4)
HALF = 512


def mm(left, right):
    return jnp.dot(left, right, preferred_element_type=F32)


def mm_nt(left, right):
    return lax.dot_general(left, right, (((1,), (1,)), ((), ())), preferred_element_type=F32)


def vmem():
    return pl.BlockSpec(memory_space=pltpu.VMEM)


def smem():
    return pl.BlockSpec(memory_space=pltpu.SMEM)


def hbm():
    return pl.BlockSpec(memory_space=pl.ANY)


def params(**extra):
    return pltpu.CompilerParams(vmem_limit_bytes=VMEM_LIMIT, **extra)


def front_kernel(info, pieces, w_stem, conv, hidden, pre_own, emb_own, stem, emb, pre):
    step = info[0]
    core = info[1]
    chip = info[2]
    block = pl.program_id(0)

    @pl.when(block == 0)
    def _():
        row = lax.broadcasted_iota(jnp.int32, (4 * BP, 4 * BP), 0)
        col = lax.broadcasted_iota(jnp.int32, (4 * BP, 4 * BP), 1)
        source = 4 * (row & (BP - 1)) + (row >> 7)
        source = jnp.where(core == 1, 4 * BP - 1 - source, source)
        stem[...] = mm((col == source).astype(BF), w_stem[...]).astype(BF)
        edge = jnp.zeros((PLANES, MARGIN, 128), F32)
        emb[:, 0:MARGIN, :] = edge
        emb[:, MARGIN + BINS : MARGIN + BINS + MARGIN, :] = edge

        def embed(block, carry):
            letters = pieces[pl.ds((WIDE // BP) * block, WIDE // BP), 0:BP, :].astype(F32).reshape(WIDE, BP)
            hot = jnp.concatenate([(letters == float(c)).astype(BF) for c in range(4)], axis=1)
            rows = mm(hot, stem[...]).astype(BF).astype(F32)
            start = pl.multiple_of(MARGIN + block * WIDE, 8)
            for plane in range(PLANES):
                emb[plane, pl.ds(start, WIDE), :] = rows[:, plane * 128 : (plane + 1) * 128]
            return carry

        lax.fori_loop(0, BINS // WIDE, embed, 0)

    base = MARGIN + block * WIDE
    for pair in range(2):
        planes = [
            [
                emb[3 * pair + third, pl.ds(base + (tap - KW // 2) * step, WIDE), :].astype(BF)
                for tap in range(KW)
            ]
            for third in range(3)
        ]
        even, odd = (
            mm(
                jnp.concatenate([planes[at + half][tap] for tap in range(KW) for half in range(2)], axis=1),
                conv[2 * pair + at],
            )
            for at in range(2)
        )
        thirds = (even[:, :128], even[:, 128:] + odd[:, :128], odd[:, 128:])
        for third in range(3):
            plane = 3 * pair + third
            x = thirds[third]
            lanes = slice(plane * 128, (plane + 1) * 128)
            pre[pl.ds(pl.multiple_of(block * WIDE, WIDE), WIDE), lanes] = x
            th = jnp.tanh(GELU_A * (x + GELU_B * (x * x * x)))
            act = 0.5 * x * (1.0 + th)
            own = emb[plane, pl.ds(pl.multiple_of(base, 8), WIDE), :]
            hidden[:, lanes] = (own + act).astype(BF)

    @pl.when(block == BINS // WIDE - 1)
    def _():
        pre_own[...] = pre[pl.ds(pl.multiple_of(chip * ROWS, ROWS), ROWS), :]
        emb_own[...] = emb[:, pl.ds(pl.multiple_of(chip * ROWS, ROWS), ROWS + 2 * MARGIN), :]


def front(info, pieces, w_stem, conv):
    return pl.pallas_call(
        front_kernel,
        out_shape=(
            jax.ShapeDtypeStruct((BINS, C), BF),
            jax.ShapeDtypeStruct((ROWS, C), F32),
            jax.ShapeDtypeStruct((PLANES, ROWS + 2 * MARGIN, 128), F32),
        ),
        grid=(BINS // WIDE,),
        in_specs=[
            smem(),
            pl.BlockSpec(pieces.shape, lambda i: (0, 0, 0)),
            pl.BlockSpec(w_stem.shape, lambda i: (0, 0)),
            pl.BlockSpec(conv.shape, lambda i: (0, 0, 0)),
        ],
        out_specs=(
            pl.BlockSpec((WIDE, C), lambda i: (i, 0)),
            pl.BlockSpec((ROWS, C), lambda i: (0, 0)),
            pl.BlockSpec((PLANES, ROWS + 2 * MARGIN, 128), lambda i: (0, 0, 0)),
        ),
        scratch_shapes=[
            pltpu.VMEM((4 * BP, C), BF),
            pltpu.VMEM((PLANES, BINS + 2 * MARGIN, 128), F32),
            pltpu.VMEM((BINS, C), F32),
        ],
        compiler_params=params(),
        cost_estimate=pl.CostEstimate(flops=2 * 10**10, bytes_accessed=10**7, transcendentals=0),
        name="front",
    )(info, pieces, w_stem, conv)


def heads_kernel(
    last, hidden, pieces, w_qkv, *refs
):
    if last:
        cot, mine, from_mine, out, wgrad = refs[:5]
    else:
        out, wgrad = refs[:2]
    q_pad, k_nat, v_nat, q_t, k_t, v_t, ga_t, x_t, scores, both, kv_sum = refs[5 if last else 2 :]

    span_rows = 1024

    def project(block, carry):
        rows = pl.ds(pl.multiple_of(block * span_rows, span_rows), span_rows)
        y = mm(hidden[rows, :], w_qkv[...])
        q_pad[rows, :] = y[:, 0:128].astype(BF)
        k_nat[rows, :] = y[:, 128 : 128 + HD].astype(BF)
        v_nat[rows, :] = y[:, 256 : 256 + HD].astype(BF)
        for at, turned in ((0, q_t), (128, k_t), (256, v_t)):
            turned[:, rows] = y[:, at : at + 128].T[0:HD].astype(BF)
        for piece in range(span_rows // BP):
            lanes = pl.ds(pl.multiple_of(block * span_rows + piece * BP, BP), BP)
            ga_t[:, lanes] = pieces[(span_rows // BP) * block + piece, BP:, :]
        return carry

    lax.fori_loop(0, BINS // span_rows, project, 0)
    kv_sum[...] = jnp.zeros_like(kv_sum)

    def span(block):
        return pl.ds(pl.multiple_of(block * ROWS, ROWS), ROWS)

    def products(slot, block):
        scores[slot] = mm(k_nat[...], q_t[:, span(block)])

    def softmax(slot):
        top = None
        for part in range(BLOCKS):
            at = slice(part * ROWS, (part + 1) * ROWS)
            most = jnp.max(scores[slot, at, :].reshape(ROWS // 8, 8, ROWS), axis=0)
            top = most if top is None else jnp.maximum(top, most)
        top = jnp.max(top, axis=0, keepdims=True)
        total = None
        for part in range(BLOCKS):
            at = slice(part * ROWS, (part + 1) * ROWS)
            e = jnp.exp2((scores[slot, at, :] - top) * (SCALE * math.log2(math.e)))
            scores[slot, at, :] = e
            some = jnp.sum(e.reshape(ROWS // 8, 8, ROWS), axis=0)
            total = some if total is None else total + some
        inverse = 1.0 / jnp.sum(total, axis=0, keepdims=True)
        for part in range(BLOCKS):
            at = slice(part * ROWS, (part + 1) * ROWS)
            both[slot, at, ROWS:] = (scores[slot, at, :] * inverse).astype(BF)
        return inverse

    def mix(slot, block):
        attn = mm(v_t[...], both[slot, :, ROWS:]).astype(BF)
        x_t[0:HD, span(block)] = attn
        return jnp.sum(ga_t[:, span(block)].astype(F32) * attn.astype(F32), axis=0, keepdims=True)

    def score_grads(slot, inverse, row_dot, block):
        gat = ga_t[:, span(block)]
        for part in range(BLOCKS // 2):
            at = slice(part * 2 * ROWS, (part + 1) * 2 * ROWS)
            gp = mm(v_nat[at, :], gat)
            both[slot, at, :ROWS] = ((scores[slot, at, :] * inverse) * (gp - row_dot)).astype(BF)

    def backward(slot, block):
        ga_pad = jnp.concatenate(
            [
                jnp.zeros((HD, ROWS), F32),
                ga_t[:, span(block)].astype(F32),
                jnp.zeros((128 - 2 * HD, ROWS), F32),
            ],
            axis=0,
        ).T.astype(BF)
        right = jnp.concatenate([q_pad[span(block), :], ga_pad], axis=0)
        x_t[HD : 2 * HD, span(block)] = (mm(k_t[...], both[slot, :, :ROWS]) * SCALE).astype(BF)
        kv_sum[...] += mm(both[slot], right)

    both[1] = jnp.zeros((BINS, 2 * ROWS), BF)
    products(0, 0)

    def attend(pair, carry):
        a, b = 2 * pair, 2 * pair + 1
        inv = softmax(0)
        backward(1, jnp.maximum(b - 2, 0))
        dot = mix(0, a)
        products(1, b)
        score_grads(0, inv, dot, a)
        inv = softmax(1)
        backward(0, a)
        dot = mix(1, b)
        products(0, jnp.minimum(b + 1, BLOCKS - 1))
        score_grads(1, inv, dot, b)
        return carry

    lax.fori_loop(0, BLOCKS // 2, attend, 0)
    backward(1, BLOCKS - 1)

    def finish(block, carry):
        rows = pl.ds(pl.multiple_of(block * ROWS, ROWS), ROWS)
        turned = kv_sum[rows, :].T
        x_t[2 * HD : 3 * HD, rows] = (turned[0:HD] * SCALE).astype(BF)
        x_t[3 * HD : 4 * HD, rows] = turned[HD : 2 * HD].astype(BF)
        out[block] = x_t[:, rows]
        return carry

    lax.fori_loop(0, BLOCKS, finish, 0)
    from_hidden = mm(x_t[HD:, :], hidden[...])
    if not last:
        wgrad[...] = from_hidden
        return
    wgrad[HD:, :] = (from_hidden + from_mine[...]).astype(BF)
    attn_mine = jnp.concatenate([mine[block, 0:HD, :] for block in range(BLOCKS)], axis=1)
    from_cot = mm(jnp.concatenate([x_t[0:HD, :], attn_mine], axis=0), cot[...])
    wgrad[0:HD, :] = (from_cot[0:HD] + from_cot[HD:]).astype(BF)


def heads(hidden, pieces, w_qkv, *before):
    last = bool(before)
    return pl.pallas_call(
        functools.partial(heads_kernel, last),
        out_shape=(
            jax.ShapeDtypeStruct((BLOCKS, 4 * HD, ROWS), BF),
            jax.ShapeDtypeStruct((4 * HD, C), BF) if last else jax.ShapeDtypeStruct((3 * HD, C), F32),
        ),
        in_specs=[vmem()] * (3 + len(before)),
        out_specs=(vmem(), vmem()),
        scratch_shapes=[
            pltpu.VMEM((BINS, 128), BF),
            pltpu.VMEM((BINS, HD), BF),
            pltpu.VMEM((BINS, HD), BF),
            pltpu.VMEM((HD, BINS), BF),
            pltpu.VMEM((HD, BINS), BF),
            pltpu.VMEM((HD, BINS), BF),
            pltpu.VMEM((HD, BINS), BF),
            pltpu.VMEM((4 * HD, BINS), BF),
            pltpu.VMEM((2, BINS, ROWS), F32),
            pltpu.VMEM((2, BINS, 2 * ROWS), BF),
            pltpu.VMEM((BINS, 128), F32),
        ],
        compiler_params=params(),
        cost_estimate=pl.CostEstimate(flops=3 * 10**10, bytes_accessed=10**7, transcendentals=0),
        name="heads",
    )(hidden, pieces, w_qkv, *before)


def tail_kernel(info, *refs):
    sources, refs = refs[:10], refs[10:]
    (out_keep, out_give, conv_keep, conv_give), refs = refs[:4], refs[4:]
    held, (branch_out, conv_grad, arrive) = refs[:10], refs[10:]
    got_same, got_cross, hidden, cot, w_out, w_query, w_key, w_value, pre, emb = held
    step = info[0]
    core = info[1]
    chip = info[2]
    loads = []
    for at in range(10):
        source = sources[at]
        if at in (2, 3):
            source = source.at[pl.ds(pl.multiple_of(chip * ROWS, ROWS), ROWS), :]
        loads.append(pltpu.make_async_copy(source, held[at], arrive.at[at]))
    for load in loads:
        load.start()
    loads[0].wait()
    loads[1].wait()
    same, cross = got_same[...], got_cross[...]
    even = jnp.where(core == 0, same, cross)
    odd = jnp.where(core == 0, cross, same)

    def rows_of(which):
        at = slice(which * HD, (which + 1) * HD)
        part = jnp.concatenate([x[chip, at] for chip in range(H // 2) for x in (even, odd)], axis=0)
        return part.astype(F32).T.astype(BF)

    for at in (2, 3, 4):
        loads[at].wait()
    branch_out[...] = hidden[...].astype(F32) + mm(rows_of(0), w_out[...])
    out_keep[...] = branch_out[pl.ds(pl.multiple_of(core * BP, BP), BP), :].astype(BF)
    out_give[...] = branch_out[pl.ds(pl.multiple_of((1 - core) * BP, BP), BP), :].astype(BF)
    grad = cot[...].astype(F32)
    for which, weight in ((1, w_query), (2, w_key), (3, w_value)):
        loads[4 + which].wait()
        grad = grad + mm_nt(rows_of(which), weight[...])
    loads[8].wait()
    loads[9].wait()
    x = pre[...]
    square = x * x
    th = jnp.tanh(GELU_A * (x + GELU_B * (square * x)))
    slope = 0.5 * (1.0 + th) + 0.5 * x * (1.0 - th * th) * (GELU_A * (1.0 + 3.0 * GELU_B * square))
    grad_t = (grad * slope).astype(BF).astype(F32).T.astype(BF)
    low = lax.broadcasted_iota(jnp.int32, (CG, 128), 1) < 64
    for tap in range(KW):
        start = MARGIN + (tap - KW // 2) * step
        planes = [emb[plane, pl.ds(start, ROWS), :].astype(BF) for plane in range(PLANES)]
        for pair in range(2):
            terms = []
            for half in range(2):
                group = 2 * pair + half
                at = WINDOWS[group]
                right = jnp.concatenate([planes[at], planes[at + 1]], axis=1)
                terms.append(mm(grad_t[group * CG : (group + 1) * CG], right))
            first, last = terms
            thirds = (first[:, :128], jnp.where(low, first[:, 128:], last[:, :128]), last[:, 128:])
            for third in range(3):
                plane = 3 * pair + third
                conv_grad[tap * CG : (tap + 1) * CG, plane * 128 : (plane + 1) * 128] = thirds[third]
    conv_grad[KW * CG :, :] = jnp.zeros((HALF * 2 - KW * CG, C), F32)
    conv_keep[...] = conv_grad[pl.ds(pl.multiple_of(core * HALF, HALF), HALF), :].astype(BF)
    conv_give[...] = conv_grad[pl.ds(pl.multiple_of((1 - core) * HALF, HALF), HALF), :].astype(BF)


def tail(info, got_same, got_cross, hidden, cot, w_out, w_query, w_key, w_value, pre, emb):
    operands = (got_same, got_cross, hidden, cot, w_out, w_query, w_key, w_value, pre, emb)
    outs = [jax.ShapeDtypeStruct(s, BF) for s in ((BP, C), (BP, C), (HALF, C), (HALF, C))]
    held = [
        pltpu.VMEM((ROWS, C) if at in (2, 3) else x.shape, x.dtype) for at, x in enumerate(operands)
    ]
    return pl.pallas_call(
        tail_kernel,
        out_shape=outs,
        in_specs=[smem()] + [hbm()] * 10,
        out_specs=[vmem()] * 4,
        scratch_shapes=held
        + [pltpu.VMEM((ROWS, C), F32), pltpu.VMEM((2 * HALF, C), F32), pltpu.SemaphoreType.DMA((10,))],
        compiler_params=params(),
        cost_estimate=pl.CostEstimate(flops=5 * 10**9, bytes_accessed=10**7, transcendentals=0),
        name="tail",
    )(info, *operands)


def unpack_weights_kernel(parts, *refs):
    outs, held, full, arrive, leave = refs[:4], refs[4], refs[5], refs[6], refs[7]
    loads = [
        pltpu.make_async_copy(parts.at[:, which * HD : (which + 1) * HD, :], held.at[which], arrive.at[which])
        for which in range(4)
    ]
    stores = [pltpu.make_async_copy(full.at[which], outs[which], leave.at[which]) for which in range(4)]
    for load in loads:
        load.start()
    for which in range(4):
        loads[which].wait()
        part = held[which].reshape(C, C).astype(F32)
        full[which] = part if which == 0 else part.T
        stores[which].start()
    for store in stores:
        store.wait()


def unpack_weights(parts):
    return pl.pallas_call(
        unpack_weights_kernel,
        out_shape=[jax.ShapeDtypeStruct((C, C), F32)] * 4,
        in_specs=[hbm()],
        out_specs=[hbm()] * 4,
        scratch_shapes=[
            pltpu.VMEM((4, H, HD, C), BF),
            pltpu.VMEM((4, C, C), F32),
            pltpu.SemaphoreType.DMA((4,)),
            pltpu.SemaphoreType.DMA((4,)),
        ],
        compiler_params=params(),
        cost_estimate=pl.CostEstimate(flops=10**7, bytes_accessed=14 * 10**6, transcendentals=0),
        name="unpack_weights",
    )(parts)


def unpack_conv_kernel(info, mine, other, out, full, turned, leave):
    core = info[1]
    full[pl.ds(pl.multiple_of(core * HALF, HALF), HALF), :] = mine[...].astype(F32)
    full[pl.ds(pl.multiple_of((1 - core) * HALF, HALF), HALF), :] = other[...].astype(F32)
    stores = [pltpu.make_async_copy(turned.at[tap], out.at[tap], leave.at[tap]) for tap in range(KW)]
    for tap in range(KW):
        turned[tap] = full[tap * CG : (tap + 1) * CG, :].T.reshape(G, CG, CG)
        stores[tap].start()
    for store in stores:
        store.wait()


def unpack_conv(info, mine, other):
    return pl.pallas_call(
        unpack_conv_kernel,
        out_shape=jax.ShapeDtypeStruct((KW, G, CG, CG), F32),
        in_specs=[smem(), vmem(), vmem()],
        out_specs=hbm(),
        scratch_shapes=[
            pltpu.VMEM((2 * HALF, C), F32),
            pltpu.VMEM((KW, G, CG, CG), F32),
            pltpu.SemaphoreType.DMA((KW,)),
        ],
        compiler_params=params(),
        cost_estimate=pl.CostEstimate(flops=10**7, bytes_accessed=5 * 10**6, transcendentals=0),
        name="unpack_conv",
    )(info, mine, other)


SWAP = [(0, 1), (1, 0)]
SEQ = ("chip", "core")
ALL_CHIPS = ("dp", "chip")


def apart(axis, bit):
    return [(i, i ^ bit) for i in range(lax.axis_size(axis))]


def to_chips(x, axes):
    return lax.all_to_all(x, axes, 0, 0, tiled=True)


def body(tokens, dilation, w_stem, conv_w, w_query, w_key, w_value, w_out, cotangent):
    core = lax.axis_index("core")
    chip = lax.axis_index("chip")
    me = lax.axis_index(SEQ)
    step = jnp.where(core == 1, -dilation[0], dilation[0])
    info = jnp.stack([step, core, chip]).astype(jnp.int32)
    own_cot = cotangent[0]
    ga_t = lax.dot_general(w_out, own_cot, (((1,), (1,)), ((), ())), preferred_element_type=F32).astype(BF)
    letters = jnp.broadcast_to(tokens.reshape(1, BP, BP).astype(BF), (H, BP, BP))
    pieces = to_chips(jnp.concatenate([letters, ga_t.reshape(H, HD, BP)], axis=1), SEQ)
    taps = conv_w.transpose(1, 0, 2, 3)
    conv = jnp.stack(
        [
            jnp.pad(taps[group], ((0, 0), (64, 0), (64, 0)) if group % 2 else ((0, 0), (0, 64), (0, 64)))
            for group in range(G)
        ]
    ).reshape(G, KW * 256, 256)
    w_qkv = jnp.concatenate(
        [
            jnp.pad(lax.dynamic_slice_in_dim(w, me * HD, HD, 1), ((0, 0), (0, 128 - HD)))
            for w in (w_query, w_key, w_value)
        ],
        axis=1,
    )
    pieces, own_cot, conv, w_qkv, info = lax.optimization_barrier((pieces, own_cot, conv, w_qkv, info))
    cot = lax.all_gather(own_cot, SEQ, axis=0, tiled=True)
    hidden, pre_own, emb_own = front(info, pieces, w_stem, conv)
    hidden_other = lax.ppermute(hidden, "core", SWAP)
    mine, from_mine = heads(hidden, pieces, w_qkv)
    got_same = to_chips(mine, "chip")
    other, wgrad = heads(hidden_other, pieces, w_qkv, cot, mine, from_mine)
    other, wgrad, got_same = lax.optimization_barrier((other, wgrad, got_same))
    got_cross = to_chips(lax.ppermute(other, "core", SWAP), "chip")
    once = lax.ppermute(wgrad, "dp", apart("dp", 1))
    wgrad = (wgrad.astype(F32) + once.astype(F32)).astype(BF)
    twice = lax.ppermute(wgrad, "dp", apart("dp", 2))
    twice, got_cross = lax.optimization_barrier((twice, got_cross))
    wgrad = (wgrad.astype(F32) + twice.astype(F32)).astype(BF)
    thrice = lax.ppermute(wgrad, "dp", apart("dp", 4))
    out_keep, out_give, conv_keep, conv_give = tail(
        info, got_same, got_cross, hidden, cot, w_out, w_query, w_key, w_value, pre_own, emb_own
    )
    thrice, conv_give, out_give = lax.optimization_barrier((thrice, conv_give, out_give))
    wgrad = (wgrad.astype(F32) + thrice.astype(F32)).astype(BF)
    wgrads = lax.all_gather(wgrad, SEQ, axis=0)
    conv_taken = lax.ppermute(conv_give, "core", SWAP)
    share = (conv_keep.astype(F32) + conv_taken.astype(F32)).astype(BF)
    parts = to_chips(share, ALL_CHIPS).reshape(64, HALF // 64, C)
    share = jnp.sum(parts.astype(F32), axis=0).astype(BF)
    conv_mine = to_chips(jnp.broadcast_to(share[None], (64, HALF // 64, C)), ALL_CHIPS).reshape(HALF, C)
    taken = lax.ppermute(out_give, "core", SWAP)
    mixed = (out_keep.astype(F32) + taken.astype(F32)).astype(BF)[None]
    conv_mine, mixed = lax.optimization_barrier((conv_mine, mixed))
    grad_conv = unpack_conv(info, conv_mine, lax.ppermute(conv_mine, "core", SWAP))
    grad_out, grad_query, grad_key, grad_value = unpack_weights(wgrads)
    return (mixed, grad_conv, grad_query, grad_key, grad_value, grad_out)


def solution(mesh):
    split = jax.sharding.Mesh(mesh.devices.reshape(8, 8, 2), ("dp", "chip", "core"))
    in_specs = (P("dp", SEQ), P("dp"), P(), P(), P(), P(), P(), P(), P("dp", SEQ, None))
    out_specs = (P("dp", SEQ, None), P(), P(), P(), P(), P())
    return jax.shard_map(body, mesh=split, in_specs=in_specs, out_specs=out_specs, check_vma=False)
```

```python
import functools
import math

import jax
import jax.numpy as jnp
from jax import lax
from jax.experimental import pallas as pl
from jax.experimental.pallas import tpu as pltpu
from jax.sharding import PartitionSpec as P

H = 16
G = 4
KW = 5
DMAX = 16
MARGIN = 2 * DMAX
C = 768
CG = C // G
HD = C // H
BP = 128
BINS = 2048
ROWS = 256
BLOCKS = BINS // ROWS
WIDE = 1024
PLANES = C // 128
PIECE = BP + HD
SCALE = HD ** (-0.5)
BF = jnp.bfloat16
F32 = jnp.float32
VMEM_LIMIT = 56 * 1024 * 1024
GELU_A = math.sqrt(2.0 / math.pi)
GELU_B = 0.044715
WINDOWS = (0, 1, 3, 4)
HALF = 512


def mm(left, right):
    return jnp.dot(left, right, preferred_element_type=F32)


def mm_nt(left, right):
    return lax.dot_general(left, right, (((1,), (1,)), ((), ())), preferred_element_type=F32)


def vmem():
    return pl.BlockSpec(memory_space=pltpu.VMEM)


def smem():
    return pl.BlockSpec(memory_space=pltpu.SMEM)


def hbm():
    return pl.BlockSpec(memory_space=pl.ANY)


def params(**extra):
    return pltpu.CompilerParams(vmem_limit_bytes=VMEM_LIMIT, **extra)


def front_kernel(info, pieces, w_stem, conv, hidden, pre_own, emb_own, stem, emb, pre):
    step = info[0]
    core = info[1]
    chip = info[2]
    block = pl.program_id(0)

    @pl.when(block == 0)
    def _():
        row = lax.broadcasted_iota(jnp.int32, (4 * BP, 4 * BP), 0)
        col = lax.broadcasted_iota(jnp.int32, (4 * BP, 4 * BP), 1)
        source = 4 * (row & (BP - 1)) + (row >> 7)
        source = jnp.where(core == 1, 4 * BP - 1 - source, source)
        stem[...] = mm((col == source).astype(BF), w_stem[...]).astype(BF)
        edge = jnp.zeros((PLANES, MARGIN, 128), F32)
        emb[:, 0:MARGIN, :] = edge
        emb[:, MARGIN + BINS : MARGIN + BINS + MARGIN, :] = edge

        def embed(block, carry):
            letters = pieces[pl.ds((WIDE // BP) * block, WIDE // BP), 0:BP, :].astype(F32).reshape(WIDE, BP)
            hot = jnp.concatenate([(letters == float(c)).astype(BF) for c in range(4)], axis=1)
            rows = mm(hot, stem[...]).astype(BF).astype(F32)
            start = pl.multiple_of(MARGIN + block * WIDE, 8)
            for plane in range(PLANES):
                emb[plane, pl.ds(start, WIDE), :] = rows[:, plane * 128 : (plane + 1) * 128]
            return carry

        lax.fori_loop(0, BINS // WIDE, embed, 0)

    base = MARGIN + block * WIDE
    for pair in range(2):
        planes = [
            [
                emb[3 * pair + third, pl.ds(base + (tap - KW // 2) * step, WIDE), :].astype(BF)
                for tap in range(KW)
            ]
            for third in range(3)
        ]
        even, odd = (
            mm(
                jnp.concatenate([planes[at + half][tap] for tap in range(KW) for half in range(2)], axis=1),
                conv[2 * pair + at],
            )
            for at in range(2)
        )
        thirds = (even[:, :128], even[:, 128:] + odd[:, :128], odd[:, 128:])
        for third in range(3):
            plane = 3 * pair + third
            x = thirds[third]
            lanes = slice(plane * 128, (plane + 1) * 128)
            pre[pl.ds(pl.multiple_of(block * WIDE, WIDE), WIDE), lanes] = x
            th = jnp.tanh(GELU_A * (x + GELU_B * (x * x * x)))
            act = 0.5 * x * (1.0 + th)
            own = emb[plane, pl.ds(pl.multiple_of(base, 8), WIDE), :]
            hidden[:, lanes] = (own + act).astype(BF)

    @pl.when(block == BINS // WIDE - 1)
    def _():
        pre_own[...] = pre[pl.ds(pl.multiple_of(chip * ROWS, ROWS), ROWS), :]
        emb_own[...] = emb[:, pl.ds(pl.multiple_of(chip * ROWS, ROWS), ROWS + 2 * MARGIN), :]


def front(info, pieces, w_stem, conv):
    return pl.pallas_call(
        front_kernel,
        out_shape=(
            jax.ShapeDtypeStruct((BINS, C), BF),
            jax.ShapeDtypeStruct((ROWS, C), F32),
            jax.ShapeDtypeStruct((PLANES, ROWS + 2 * MARGIN, 128), F32),
        ),
        grid=(BINS // WIDE,),
        in_specs=[
            smem(),
            pl.BlockSpec(pieces.shape, lambda i: (0, 0, 0)),
            pl.BlockSpec(w_stem.shape, lambda i: (0, 0)),
            pl.BlockSpec(conv.shape, lambda i: (0, 0, 0)),
        ],
        out_specs=(
            pl.BlockSpec((WIDE, C), lambda i: (i, 0)),
            pl.BlockSpec((ROWS, C), lambda i: (0, 0)),
            pl.BlockSpec((PLANES, ROWS + 2 * MARGIN, 128), lambda i: (0, 0, 0)),
        ),
        scratch_shapes=[
            pltpu.VMEM((4 * BP, C), BF),
            pltpu.VMEM((PLANES, BINS + 2 * MARGIN, 128), F32),
            pltpu.VMEM((BINS, C), F32),
        ],
        compiler_params=params(),
        cost_estimate=pl.CostEstimate(flops=2 * 10**10, bytes_accessed=10**7, transcendentals=0),
        name="front",
    )(info, pieces, w_stem, conv)


def heads_kernel(
    last, hidden, pieces, w_qkv, *refs
):
    if last:
        cot, mine, from_mine, out, wgrad = refs[:5]
    else:
        out, wgrad = refs[:2]
    q_pad, k_nat, v_nat, q_t, k_t, v_t, ga_t, x_t, scores, both, kv_sum = refs[5 if last else 2 :]

    span_rows = 1024

    def project(block, carry):
        rows = pl.ds(pl.multiple_of(block * span_rows, span_rows), span_rows)
        y = mm(hidden[rows, :], w_qkv[...])
        q_pad[rows, :] = y[:, 0:128].astype(BF)
        k_nat[rows, :] = y[:, 128 : 128 + HD].astype(BF)
        v_nat[rows, :] = y[:, 256 : 256 + HD].astype(BF)
        for at, turned in ((0, q_t), (128, k_t), (256, v_t)):
            turned[:, rows] = y[:, at : at + 128].T[0:HD].astype(BF)
        for piece in range(span_rows // BP):
            lanes = pl.ds(pl.multiple_of(block * span_rows + piece * BP, BP), BP)
            ga_t[:, lanes] = pieces[(span_rows // BP) * block + piece, BP:, :]
        return carry

    lax.fori_loop(0, BINS // span_rows, project, 0)
    kv_sum[...] = jnp.zeros_like(kv_sum)

    def span(block):
        return pl.ds(pl.multiple_of(block * ROWS, ROWS), ROWS)

    def products(slot, block):
        scores[slot] = mm(k_nat[...], q_t[:, span(block)])

    def softmax(slot):
        top = None
        for part in range(BLOCKS):
            at = slice(part * ROWS, (part + 1) * ROWS)
            most = jnp.max(scores[slot, at, :].reshape(ROWS // 8, 8, ROWS), axis=0)
            top = most if top is None else jnp.maximum(top, most)
        top = jnp.max(top, axis=0, keepdims=True)
        total = None
        for part in range(BLOCKS):
            at = slice(part * ROWS, (part + 1) * ROWS)
            e = jnp.exp2((scores[slot, at, :] - top) * (SCALE * math.log2(math.e)))
            scores[slot, at, :] = e
            some = jnp.sum(e.reshape(ROWS // 8, 8, ROWS), axis=0)
            total = some if total is None else total + some
        inverse = 1.0 / jnp.sum(total, axis=0, keepdims=True)
        for part in range(BLOCKS):
            at = slice(part * ROWS, (part + 1) * ROWS)
            both[slot, at, ROWS:] = (scores[slot, at, :] * inverse).astype(BF)
        return inverse

    def mix(slot, block):
        attn = mm(v_t[...], both[slot, :, ROWS:]).astype(BF)
        x_t[0:HD, span(block)] = attn
        return jnp.sum(ga_t[:, span(block)].astype(F32) * attn.astype(F32), axis=0, keepdims=True)

    def score_grads(slot, inverse, row_dot, block):
        gat = ga_t[:, span(block)]
        for part in range(BLOCKS // 2):
            at = slice(part * 2 * ROWS, (part + 1) * 2 * ROWS)
            gp = mm(v_nat[at, :], gat)
            both[slot, at, :ROWS] = ((scores[slot, at, :] * inverse) * (gp - row_dot)).astype(BF)

    def backward(slot, block):
        ga_pad = jnp.concatenate(
            [
                jnp.zeros((HD, ROWS), F32),
                ga_t[:, span(block)].astype(F32),
                jnp.zeros((128 - 2 * HD, ROWS), F32),
            ],
            axis=0,
        ).T.astype(BF)
        right = jnp.concatenate([q_pad[span(block), :], ga_pad], axis=0)
        x_t[HD : 2 * HD, span(block)] = (mm(k_t[...], both[slot, :, :ROWS]) * SCALE).astype(BF)
        kv_sum[...] += mm(both[slot], right)

    both[1] = jnp.zeros((BINS, 2 * ROWS), BF)
    products(0, 0)

    def attend(pair, carry):
        a, b = 2 * pair, 2 * pair + 1
        inv = softmax(0)
        backward(1, jnp.maximum(b - 2, 0))
        dot = mix(0, a)
        products(1, b)
        score_grads(0, inv, dot, a)
        inv = softmax(1)
        backward(0, a)
        dot = mix(1, b)
        products(0, jnp.minimum(b + 1, BLOCKS - 1))
        score_grads(1, inv, dot, b)
        return carry

    lax.fori_loop(0, BLOCKS // 2, attend, 0)
    backward(1, BLOCKS - 1)

    def finish(block, carry):
        rows = pl.ds(pl.multiple_of(block * ROWS, ROWS), ROWS)
        turned = kv_sum[rows, :].T
        x_t[2 * HD : 3 * HD, rows] = (turned[0:HD] * SCALE).astype(BF)
        x_t[3 * HD : 4 * HD, rows] = turned[HD : 2 * HD].astype(BF)
        out[block] = x_t[:, rows]
        return carry

    lax.fori_loop(0, BLOCKS, finish, 0)
    from_hidden = mm(x_t[HD:, :], hidden[...])
    if not last:
        wgrad[...] = from_hidden
        return
    wgrad[HD:, :] = (from_hidden + from_mine[...]).astype(BF)
    attn_mine = jnp.concatenate([mine[block, 0:HD, :] for block in range(BLOCKS)], axis=1)
    from_cot = mm(jnp.concatenate([x_t[0:HD, :], attn_mine], axis=0), cot[...])
    wgrad[0:HD, :] = (from_cot[0:HD] + from_cot[HD:]).astype(BF)


def heads(hidden, pieces, w_qkv, *before):
    last = bool(before)
    return pl.pallas_call(
        functools.partial(heads_kernel, last),
        out_shape=(
            jax.ShapeDtypeStruct((BLOCKS, 4 * HD, ROWS), BF),
            jax.ShapeDtypeStruct((4 * HD, C), BF) if last else jax.ShapeDtypeStruct((3 * HD, C), F32),
        ),
        in_specs=[vmem()] * (3 + len(before)),
        out_specs=(vmem(), vmem()),
        scratch_shapes=[
            pltpu.VMEM((BINS, 128), BF),
            pltpu.VMEM((BINS, HD), BF),
            pltpu.VMEM((BINS, HD), BF),
            pltpu.VMEM((HD, BINS), BF),
            pltpu.VMEM((HD, BINS), BF),
            pltpu.VMEM((HD, BINS), BF),
            pltpu.VMEM((HD, BINS), BF),
            pltpu.VMEM((4 * HD, BINS), BF),
            pltpu.VMEM((2, BINS, ROWS), F32),
            pltpu.VMEM((2, BINS, 2 * ROWS), BF),
            pltpu.VMEM((BINS, 128), F32),
        ],
        compiler_params=params(),
        cost_estimate=pl.CostEstimate(flops=3 * 10**10, bytes_accessed=10**7, transcendentals=0),
        name="heads",
    )(hidden, pieces, w_qkv, *before)


def tail_kernel(info, *refs):
    sources, refs = refs[:10], refs[10:]
    (out_keep, out_give, conv_keep, conv_give), refs = refs[:4], refs[4:]
    held, (branch_out, conv_grad, arrive) = refs[:10], refs[10:]
    got_same, got_cross, hidden, cot, w_out, w_query, w_key, w_value, pre, emb = held
    step = info[0]
    core = info[1]
    chip = info[2]
    loads = []
    for at in range(10):
        source = sources[at]
        if at in (2, 3):
            source = source.at[pl.ds(pl.multiple_of(chip * ROWS, ROWS), ROWS), :]
        loads.append(pltpu.make_async_copy(source, held[at], arrive.at[at]))
    for load in loads:
        load.start()
    loads[0].wait()
    loads[1].wait()
    same, cross = got_same[...], got_cross[...]
    even = jnp.where(core == 0, same, cross)
    odd = jnp.where(core == 0, cross, same)

    def rows_of(which):
        at = slice(which * HD, (which + 1) * HD)
        part = jnp.concatenate([x[chip, at] for chip in range(H // 2) for x in (even, odd)], axis=0)
        return part.astype(F32).T.astype(BF)

    for at in (2, 3, 4):
        loads[at].wait()
    branch_out[...] = hidden[...].astype(F32) + mm(rows_of(0), w_out[...])
    out_keep[...] = branch_out[pl.ds(pl.multiple_of(core * BP, BP), BP), :].astype(BF)
    out_give[...] = branch_out[pl.ds(pl.multiple_of((1 - core) * BP, BP), BP), :].astype(BF)
    grad = cot[...].astype(F32)
    for which, weight in ((1, w_query), (2, w_key), (3, w_value)):
        loads[4 + which].wait()
        grad = grad + mm_nt(rows_of(which), weight[...])
    loads[8].wait()
    loads[9].wait()
    x = pre[...]
    square = x * x
    th = jnp.tanh(GELU_A * (x + GELU_B * (square * x)))
    slope = 0.5 * (1.0 + th) + 0.5 * x * (1.0 - th * th) * (GELU_A * (1.0 + 3.0 * GELU_B * square))
    grad_t = (grad * slope).astype(BF).astype(F32).T.astype(BF)
    low = lax.broadcasted_iota(jnp.int32, (CG, 128), 1) < 64
    for tap in range(KW):
        start = MARGIN + (tap - KW // 2) * step
        planes = [emb[plane, pl.ds(start, ROWS), :].astype(BF) for plane in range(PLANES)]
        for pair in range(2):
            terms = []
            for half in range(2):
                group = 2 * pair + half
                at = WINDOWS[group]
                right = jnp.concatenate([planes[at], planes[at + 1]], axis=1)
                terms.append(mm(grad_t[group * CG : (group + 1) * CG], right))
            first, last = terms
            thirds = (first[:, :128], jnp.where(low, first[:, 128:], last[:, :128]), last[:, 128:])
            for third in range(3):
                plane = 3 * pair + third
                conv_grad[tap * CG : (tap + 1) * CG, plane * 128 : (plane + 1) * 128] = thirds[third]
    conv_grad[KW * CG :, :] = jnp.zeros((HALF * 2 - KW * CG, C), F32)
    conv_keep[...] = conv_grad[pl.ds(pl.multiple_of(core * HALF, HALF), HALF), :].astype(BF)
    conv_give[...] = conv_grad[pl.ds(pl.multiple_of((1 - core) * HALF, HALF), HALF), :].astype(BF)


def tail(info, got_same, got_cross, hidden, cot, w_out, w_query, w_key, w_value, pre, emb):
    operands = (got_same, got_cross, hidden, cot, w_out, w_query, w_key, w_value, pre, emb)
    outs = [jax.ShapeDtypeStruct(s, BF) for s in ((BP, C), (BP, C), (HALF, C), (HALF, C))]
    held = [
        pltpu.VMEM((ROWS, C) if at in (2, 3) else x.shape, x.dtype) for at, x in enumerate(operands)
    ]
    return pl.pallas_call(
        tail_kernel,
        out_shape=outs,
        in_specs=[smem()] + [hbm()] * 10,
        out_specs=[vmem()] * 4,
        scratch_shapes=held
        + [pltpu.VMEM((ROWS, C), F32), pltpu.VMEM((2 * HALF, C), F32), pltpu.SemaphoreType.DMA((10,))],
        compiler_params=params(),
        cost_estimate=pl.CostEstimate(flops=5 * 10**9, bytes_accessed=10**7, transcendentals=0),
        name="tail",
    )(info, *operands)


def unpack_kernel(info, mine, other, parts, *refs):
    conv_out, outs, refs = refs[0], refs[1:5], refs[5:]
    halves, turned, held, full, arrive, leave = refs
    core = info[1]
    loads = [
        pltpu.make_async_copy(mine, halves.at[core], arrive.at[4]),
        pltpu.make_async_copy(other, halves.at[1 - core], arrive.at[5]),
    ]
    for which in range(4):
        at = slice(which * HD, (which + 1) * HD)
        loads.append(pltpu.make_async_copy(parts.at[:, at, :], held.at[which], arrive.at[which]))
    for load in loads:
        load.start()
    stores = [pltpu.make_async_copy(turned.at[tap], conv_out.at[tap], leave.at[4 + tap]) for tap in range(KW)]
    stores += [pltpu.make_async_copy(full.at[which], outs[which], leave.at[which]) for which in range(4)]
    loads[0].wait()
    loads[1].wait()
    rows = halves[...].reshape(2 * HALF, C)
    for tap in range(KW):
        turned[tap] = rows[tap * CG : (tap + 1) * CG, :].astype(F32).T.reshape(G, CG, CG)
        stores[tap].start()
    for which in range(4):
        loads[2 + which].wait()
        part = held[which].reshape(C, C).astype(F32)
        full[which] = part if which == 0 else part.T
        stores[KW + which].start()
    for store in stores:
        store.wait()


def unpack(info, mine, other, parts):
    return pl.pallas_call(
        unpack_kernel,
        out_shape=[jax.ShapeDtypeStruct((KW, G, CG, CG), F32)] + [jax.ShapeDtypeStruct((C, C), F32)] * 4,
        in_specs=[smem()] + [hbm()] * 3,
        out_specs=[hbm()] * 5,
        scratch_shapes=[
            pltpu.VMEM((2, HALF, C), BF),
            pltpu.VMEM((KW, G, CG, CG), F32),
            pltpu.VMEM((4, H, HD, C), BF),
            pltpu.VMEM((4, C, C), F32),
            pltpu.SemaphoreType.DMA((6,)),
            pltpu.SemaphoreType.DMA((4 + KW,)),
        ],
        compiler_params=params(),
        cost_estimate=pl.CostEstimate(flops=10**7, bytes_accessed=20 * 10**6, transcendentals=0),
        name="unpack",
    )(info, mine, other, parts)


SWAP = [(0, 1), (1, 0)]
SEQ = ("chip", "core")
ALL_CHIPS = ("dp", "chip")


def apart(axis, bit):
    return [(i, i ^ bit) for i in range(lax.axis_size(axis))]


def to_chips(x, axes):
    return lax.all_to_all(x, axes, 0, 0, tiled=True)


def body(tokens, dilation, w_stem, conv_w, w_query, w_key, w_value, w_out, cotangent):
    core = lax.axis_index("core")
    chip = lax.axis_index("chip")
    me = lax.axis_index(SEQ)
    step = jnp.where(core == 1, -dilation[0], dilation[0])
    info = jnp.stack([step, core, chip]).astype(jnp.int32)
    own_cot = cotangent[0]
    ga_t = lax.dot_general(w_out, own_cot, (((1,), (1,)), ((), ())), preferred_element_type=F32).astype(BF)
    letters = jnp.broadcast_to(tokens.reshape(1, BP, BP).astype(BF), (H, BP, BP))
    pieces = to_chips(jnp.concatenate([letters, ga_t.reshape(H, HD, BP)], axis=1), SEQ)
    taps = conv_w.transpose(1, 0, 2, 3)
    conv = jnp.stack(
        [
            jnp.pad(taps[group], ((0, 0), (64, 0), (64, 0)) if group % 2 else ((0, 0), (0, 64), (0, 64)))
            for group in range(G)
        ]
    ).reshape(G, KW * 256, 256)
    w_qkv = jnp.concatenate(
        [
            jnp.pad(lax.dynamic_slice_in_dim(w, me * HD, HD, 1), ((0, 0), (0, 128 - HD)))
            for w in (w_query, w_key, w_value)
        ],
        axis=1,
    )
    pieces, own_cot, conv, w_qkv, info = lax.optimization_barrier((pieces, own_cot, conv, w_qkv, info))
    cot = lax.all_gather(own_cot, SEQ, axis=0, tiled=True)
    hidden, pre_own, emb_own = front(info, pieces, w_stem, conv)
    hidden_other = lax.ppermute(hidden, "core", SWAP)
    mine, from_mine = heads(hidden, pieces, w_qkv)
    got_same = to_chips(mine, "chip")
    other, wgrad = heads(hidden_other, pieces, w_qkv, cot, mine, from_mine)
    other, wgrad, got_same = lax.optimization_barrier((other, wgrad, got_same))
    got_cross = to_chips(lax.ppermute(other, "core", SWAP), "chip")
    once = lax.ppermute(wgrad, "dp", apart("dp", 1))
    wgrad = (wgrad.astype(F32) + once.astype(F32)).astype(BF)
    twice = lax.ppermute(wgrad, "dp", apart("dp", 2))
    twice, got_cross = lax.optimization_barrier((twice, got_cross))
    wgrad = (wgrad.astype(F32) + twice.astype(F32)).astype(BF)
    thrice = lax.ppermute(wgrad, "dp", apart("dp", 4))
    out_keep, out_give, conv_keep, conv_give = tail(
        info, got_same, got_cross, hidden, cot, w_out, w_query, w_key, w_value, pre_own, emb_own
    )
    thrice, conv_give, out_give = lax.optimization_barrier((thrice, conv_give, out_give))
    wgrad = (wgrad.astype(F32) + thrice.astype(F32)).astype(BF)
    wgrads = lax.all_gather(wgrad, SEQ, axis=0)
    conv_taken = lax.ppermute(conv_give, "core", SWAP)
    share = (conv_keep.astype(F32) + conv_taken.astype(F32)).astype(BF)
    parts = to_chips(share, ALL_CHIPS).reshape(64, HALF // 64, C)
    share = jnp.sum(parts.astype(F32), axis=0).astype(BF)
    conv_mine = to_chips(jnp.broadcast_to(share[None], (64, HALF // 64, C)), ALL_CHIPS).reshape(HALF, C)
    taken = lax.ppermute(out_give, "core", SWAP)
    mixed = (out_keep.astype(F32) + taken.astype(F32)).astype(BF)[None]
    conv_mine, mixed = lax.optimization_barrier((conv_mine, mixed))
    grad_conv, grad_out, grad_query, grad_key, grad_value = unpack(
        info, conv_mine, lax.ppermute(conv_mine, "core", SWAP), wgrads
    )
    return (mixed, grad_conv, grad_query, grad_key, grad_value, grad_out)


def solution(mesh):
    split = jax.sharding.Mesh(mesh.devices.reshape(8, 8, 2), ("dp", "chip", "core"))
    in_specs = (P("dp", SEQ), P("dp"), P(), P(), P(), P(), P(), P(), P("dp", SEQ, None))
    out_specs = (P("dp", SEQ, None), P(), P(), P(), P(), P())
    return jax.shard_map(body, mesh=split, in_specs=in_specs, out_specs=out_specs, check_vma=False)
```

```python
import functools
import math

import jax
import jax.numpy as jnp
from jax import lax
from jax.experimental import pallas as pl
from jax.experimental.pallas import tpu as pltpu
from jax.sharding import PartitionSpec as P

H = 16
G = 4
KW = 5
DMAX = 16
MARGIN = 2 * DMAX
C = 768
CG = C // G
HD = C // H
BP = 128
BINS = 2048
ROWS = 256
BLOCKS = BINS // ROWS
WIDE = 1024
PLANES = C // 128
PIECE = BP + HD
SCALE = HD ** (-0.5)
BF = jnp.bfloat16
F32 = jnp.float32
VMEM_LIMIT = 56 * 1024 * 1024
GELU_A = math.sqrt(2.0 / math.pi)
GELU_B = 0.044715
WINDOWS = (0, 1, 3, 4)
HALF = 512


def mm(left, right):
    return jnp.dot(left, right, preferred_element_type=F32)


def mm_nt(left, right):
    return lax.dot_general(left, right, (((1,), (1,)), ((), ())), preferred_element_type=F32)


def vmem():
    return pl.BlockSpec(memory_space=pltpu.VMEM)


def smem():
    return pl.BlockSpec(memory_space=pltpu.SMEM)


def hbm():
    return pl.BlockSpec(memory_space=pl.ANY)


def params(**extra):
    return pltpu.CompilerParams(vmem_limit_bytes=VMEM_LIMIT, **extra)


def front_kernel(info, pieces, w_stem, conv, hidden, pre_own, emb_own, stem, emb, pre):
    step = info[0]
    core = info[1]
    chip = info[2]
    block = pl.program_id(0)

    @pl.when(block == 0)
    def _():
        row = lax.broadcasted_iota(jnp.int32, (4 * BP, 4 * BP), 0)
        col = lax.broadcasted_iota(jnp.int32, (4 * BP, 4 * BP), 1)
        source = 4 * (row & (BP - 1)) + (row >> 7)
        source = jnp.where(core == 1, 4 * BP - 1 - source, source)
        stem[...] = mm((col == source).astype(BF), w_stem[...]).astype(BF)
        edge = jnp.zeros((PLANES, MARGIN, 128), F32)
        emb[:, 0:MARGIN, :] = edge
        emb[:, MARGIN + BINS : MARGIN + BINS + MARGIN, :] = edge

        def embed(block, carry):
            letters = pieces[pl.ds((WIDE // BP) * block, WIDE // BP), 0:BP, :].astype(F32).reshape(WIDE, BP)
            hot = jnp.concatenate([(letters == float(c)).astype(BF) for c in range(4)], axis=1)
            rows = mm(hot, stem[...]).astype(BF).astype(F32)
            start = pl.multiple_of(MARGIN + block * WIDE, 8)
            for plane in range(PLANES):
                emb[plane, pl.ds(start, WIDE), :] = rows[:, plane * 128 : (plane + 1) * 128]
            return carry

        lax.fori_loop(0, BINS // WIDE, embed, 0)

    base = MARGIN + block * WIDE
    for pair in range(2):
        planes = [
            [
                emb[3 * pair + third, pl.ds(base + (tap - KW // 2) * step, WIDE), :].astype(BF)
                for tap in range(KW)
            ]
            for third in range(3)
        ]
        even, odd = (
            mm(
                jnp.concatenate([planes[at + half][tap] for tap in range(KW) for half in range(2)], axis=1),
                conv[2 * pair + at],
            )
            for at in range(2)
        )
        thirds = (even[:, :128], even[:, 128:] + odd[:, :128], odd[:, 128:])
        for third in range(3):
            plane = 3 * pair + third
            x = thirds[third]
            lanes = slice(plane * 128, (plane + 1) * 128)
            pre[pl.ds(pl.multiple_of(block * WIDE, WIDE), WIDE), lanes] = x
            th = jnp.tanh(GELU_A * (x + GELU_B * (x * x * x)))
            act = 0.5 * x * (1.0 + th)
            own = emb[plane, pl.ds(pl.multiple_of(base, 8), WIDE), :]
            hidden[:, lanes] = (own + act).astype(BF)

    @pl.when(block == BINS // WIDE - 1)
    def _():
        pre_own[...] = pre[pl.ds(pl.multiple_of(chip * ROWS, ROWS), ROWS), :]
        emb_own[...] = emb[:, pl.ds(pl.multiple_of(chip * ROWS, ROWS), ROWS + 2 * MARGIN), :]


def front(info, pieces, w_stem, conv):
    return pl.pallas_call(
        front_kernel,
        out_shape=(
            jax.ShapeDtypeStruct((BINS, C), BF),
            jax.ShapeDtypeStruct((ROWS, C), F32),
            jax.ShapeDtypeStruct((PLANES, ROWS + 2 * MARGIN, 128), F32),
        ),
        grid=(BINS // WIDE,),
        in_specs=[
            smem(),
            pl.BlockSpec(pieces.shape, lambda i: (0, 0, 0)),
            pl.BlockSpec(w_stem.shape, lambda i: (0, 0)),
            pl.BlockSpec(conv.shape, lambda i: (0, 0, 0)),
        ],
        out_specs=(
            pl.BlockSpec((WIDE, C), lambda i: (i, 0)),
            pl.BlockSpec((ROWS, C), lambda i: (0, 0)),
            pl.BlockSpec((PLANES, ROWS + 2 * MARGIN, 128), lambda i: (0, 0, 0)),
        ),
        scratch_shapes=[
            pltpu.VMEM((4 * BP, C), BF),
            pltpu.VMEM((PLANES, BINS + 2 * MARGIN, 128), F32),
            pltpu.VMEM((BINS, C), F32),
        ],
        compiler_params=params(),
        cost_estimate=pl.CostEstimate(flops=2 * 10**10, bytes_accessed=10**7, transcendentals=0),
        name="front",
    )(info, pieces, w_stem, conv)


def heads_kernel(
    last, hidden, pieces, w_qkv, *refs
):
    if last:
        cot, mine, from_mine, out, wgrad = refs[:5]
    else:
        out, wgrad = refs[:2]
    q_pad, k_nat, v_nat, q_t, k_t, v_t, ga_t, x_t, scores, both, kv_sum = refs[5 if last else 2 :]

    span_rows = 1024

    def project(block, carry):
        rows = pl.ds(pl.multiple_of(block * span_rows, span_rows), span_rows)
        y = mm(hidden[rows, :], w_qkv[...])
        q_pad[rows, :] = y[:, 0:128].astype(BF)
        k_nat[rows, :] = y[:, 128 : 128 + HD].astype(BF)
        v_nat[rows, :] = y[:, 256 : 256 + HD].astype(BF)
        for at, turned in ((0, q_t), (128, k_t), (256, v_t)):
            turned[:, rows] = y[:, at : at + 128].T[0:HD].astype(BF)
        for piece in range(span_rows // BP):
            lanes = pl.ds(pl.multiple_of(block * span_rows + piece * BP, BP), BP)
            ga_t[:, lanes] = pieces[(span_rows // BP) * block + piece, BP:, :]
        return carry

    lax.fori_loop(0, BINS // span_rows, project, 0)
    kv_sum[...] = jnp.zeros_like(kv_sum)

    def span(block):
        return pl.ds(pl.multiple_of(block * ROWS, ROWS), ROWS)

    def products(slot, block):
        scores[slot] = mm(k_nat[...], q_t[:, span(block)])

    def softmax(slot):
        top = None
        for part in range(BLOCKS):
            at = slice(part * ROWS, (part + 1) * ROWS)
            most = jnp.max(scores[slot, at, :].reshape(ROWS // 8, 8, ROWS), axis=0)
            top = most if top is None else jnp.maximum(top, most)
        top = jnp.max(top, axis=0, keepdims=True)
        total = None
        for part in range(BLOCKS):
            at = slice(part * ROWS, (part + 1) * ROWS)
            e = jnp.exp2((scores[slot, at, :] - top) * (SCALE * math.log2(math.e)))
            scores[slot, at, :] = e
            some = jnp.sum(e.reshape(ROWS // 8, 8, ROWS), axis=0)
            total = some if total is None else total + some
        inverse = 1.0 / jnp.sum(total, axis=0, keepdims=True)
        for part in range(BLOCKS):
            at = slice(part * ROWS, (part + 1) * ROWS)
            both[slot, at, ROWS:] = (scores[slot, at, :] * inverse).astype(BF)
        return inverse

    def mix(slot, block):
        attn = mm(v_t[...], both[slot, :, ROWS:]).astype(BF)
        x_t[0:HD, span(block)] = attn
        return jnp.sum(ga_t[:, span(block)].astype(F32) * attn.astype(F32), axis=0, keepdims=True)

    def score_grads(slot, inverse, row_dot, block):
        gat = ga_t[:, span(block)]
        for part in range(BLOCKS // 2):
            at = slice(part * 2 * ROWS, (part + 1) * 2 * ROWS)
            gp = mm(v_nat[at, :], gat)
            both[slot, at, :ROWS] = ((scores[slot, at, :] * inverse) * (gp - row_dot)).astype(BF)

    def backward(slot, block):
        ga_pad = jnp.concatenate(
            [
                jnp.zeros((HD, ROWS), F32),
                ga_t[:, span(block)].astype(F32),
                jnp.zeros((128 - 2 * HD, ROWS), F32),
            ],
            axis=0,
        ).T.astype(BF)
        right = jnp.concatenate([q_pad[span(block), :], ga_pad], axis=0)
        x_t[HD : 2 * HD, span(block)] = (mm(k_t[...], both[slot, :, :ROWS]) * SCALE).astype(BF)
        kv_sum[...] += mm(both[slot], right)

    both[1] = jnp.zeros((BINS, 2 * ROWS), BF)
    products(0, 0)

    def attend(pair, carry):
        a, b = 2 * pair, 2 * pair + 1
        backward(1, jnp.maximum(b - 2, 0))
        inv = softmax(0)
        products(1, b)
        dot = mix(0, a)
        score_grads(0, inv, dot, a)
        backward(0, a)
        inv = softmax(1)
        products(0, jnp.minimum(b + 1, BLOCKS - 1))
        dot = mix(1, b)
        score_grads(1, inv, dot, b)
        return carry

    lax.fori_loop(0, BLOCKS // 2, attend, 0)
    backward(1, BLOCKS - 1)

    def finish(block, carry):
        rows = pl.ds(pl.multiple_of(block * ROWS, ROWS), ROWS)
        turned = kv_sum[rows, :].T
        x_t[2 * HD : 3 * HD, rows] = (turned[0:HD] * SCALE).astype(BF)
        x_t[3 * HD : 4 * HD, rows] = turned[HD : 2 * HD].astype(BF)
        out[block] = x_t[:, rows]
        return carry

    lax.fori_loop(0, BLOCKS, finish, 0)
    from_hidden = mm(x_t[HD:, :], hidden[...])
    if not last:
        wgrad[...] = from_hidden
        return
    wgrad[HD:, :] = (from_hidden + from_mine[...]).astype(BF)
    attn_mine = jnp.concatenate([mine[block, 0:HD, :] for block in range(BLOCKS)], axis=1)
    from_cot = mm(jnp.concatenate([x_t[0:HD, :], attn_mine], axis=0), cot[...])
    wgrad[0:HD, :] = (from_cot[0:HD] + from_cot[HD:]).astype(BF)


def heads(hidden, pieces, w_qkv, *before):
    last = bool(before)
    return pl.pallas_call(
        functools.partial(heads_kernel, last),
        out_shape=(
            jax.ShapeDtypeStruct((BLOCKS, 4 * HD, ROWS), BF),
            jax.ShapeDtypeStruct((4 * HD, C), BF) if last else jax.ShapeDtypeStruct((3 * HD, C), F32),
        ),
        in_specs=[vmem()] * (3 + len(before)),
        out_specs=(vmem(), vmem()),
        scratch_shapes=[
            pltpu.VMEM((BINS, 128), BF),
            pltpu.VMEM((BINS, HD), BF),
            pltpu.VMEM((BINS, HD), BF),
            pltpu.VMEM((HD, BINS), BF),
            pltpu.VMEM((HD, BINS), BF),
            pltpu.VMEM((HD, BINS), BF),
            pltpu.VMEM((HD, BINS), BF),
            pltpu.VMEM((4 * HD, BINS), BF),
            pltpu.VMEM((2, BINS, ROWS), F32),
            pltpu.VMEM((2, BINS, 2 * ROWS), BF),
            pltpu.VMEM((BINS, 128), F32),
        ],
        compiler_params=params(),
        cost_estimate=pl.CostEstimate(flops=3 * 10**10, bytes_accessed=10**7, transcendentals=0),
        name="heads",
    )(hidden, pieces, w_qkv, *before)


def tail_kernel(info, *refs):
    sources, refs = refs[:10], refs[10:]
    (out_keep, out_give, conv_keep, conv_give), refs = refs[:4], refs[4:]
    held, (branch_out, conv_grad, arrive) = refs[:10], refs[10:]
    got_same, got_cross, hidden, cot, w_out, w_query, w_key, w_value, pre, emb = held
    step = info[0]
    core = info[1]
    chip = info[2]
    loads = []
    for at in range(10):
        source = sources[at]
        if at in (2, 3):
            source = source.at[pl.ds(pl.multiple_of(chip * ROWS, ROWS), ROWS), :]
        loads.append(pltpu.make_async_copy(source, held[at], arrive.at[at]))
    for load in loads:
        load.start()
    loads[0].wait()
    loads[1].wait()
    same, cross = got_same[...], got_cross[...]
    even = jnp.where(core == 0, same, cross)
    odd = jnp.where(core == 0, cross, same)

    def rows_of(which):
        at = slice(which * HD, (which + 1) * HD)
        part = jnp.concatenate([x[chip, at] for chip in range(H // 2) for x in (even, odd)], axis=0)
        return part.astype(F32).T.astype(BF)

    for at in (2, 3, 4):
        loads[at].wait()
    branch_out[...] = hidden[...].astype(F32) + mm(rows_of(0), w_out[...])
    out_keep[...] = branch_out[pl.ds(pl.multiple_of(core * BP, BP), BP), :].astype(BF)
    out_give[...] = branch_out[pl.ds(pl.multiple_of((1 - core) * BP, BP), BP), :].astype(BF)
    grad = cot[...].astype(F32)
    for which, weight in ((1, w_query), (2, w_key), (3, w_value)):
        loads[4 + which].wait()
        grad = grad + mm_nt(rows_of(which), weight[...])
    loads[8].wait()
    loads[9].wait()
    x = pre[...]
    square = x * x
    th = jnp.tanh(GELU_A * (x + GELU_B * (square * x)))
    slope = 0.5 * (1.0 + th) + 0.5 * x * (1.0 - th * th) * (GELU_A * (1.0 + 3.0 * GELU_B * square))
    grad_t = (grad * slope).astype(BF).astype(F32).T.astype(BF)
    low = lax.broadcasted_iota(jnp.int32, (CG, 128), 1) < 64
    for tap in range(KW):
        start = MARGIN + (tap - KW // 2) * step
        planes = [emb[plane, pl.ds(start, ROWS), :].astype(BF) for plane in range(PLANES)]
        for pair in range(2):
            terms = []
            for half in range(2):
                group = 2 * pair + half
                at = WINDOWS[group]
                right = jnp.concatenate([planes[at], planes[at + 1]], axis=1)
                terms.append(mm(grad_t[group * CG : (group + 1) * CG], right))
            first, last = terms
            thirds = (first[:, :128], jnp.where(low, first[:, 128:], last[:, :128]), last[:, 128:])
            for third in range(3):
                plane = 3 * pair + third
                conv_grad[tap * CG : (tap + 1) * CG, plane * 128 : (plane + 1) * 128] = thirds[third]
    conv_grad[KW * CG :, :] = jnp.zeros((HALF * 2 - KW * CG, C), F32)
    conv_keep[...] = conv_grad[pl.ds(pl.multiple_of(core * HALF, HALF), HALF), :].astype(BF)
    conv_give[...] = conv_grad[pl.ds(pl.multiple_of((1 - core) * HALF, HALF), HALF), :].astype(BF)


def tail(info, got_same, got_cross, hidden, cot, w_out, w_query, w_key, w_value, pre, emb):
    operands = (got_same, got_cross, hidden, cot, w_out, w_query, w_key, w_value, pre, emb)
    outs = [jax.ShapeDtypeStruct(s, BF) for s in ((BP, C), (BP, C), (HALF, C), (HALF, C))]
    held = [
        pltpu.VMEM((ROWS, C) if at in (2, 3) else x.shape, x.dtype) for at, x in enumerate(operands)
    ]
    return pl.pallas_call(
        tail_kernel,
        out_shape=outs,
        in_specs=[smem()] + [hbm()] * 10,
        out_specs=[vmem()] * 4,
        scratch_shapes=held
        + [pltpu.VMEM((ROWS, C), F32), pltpu.VMEM((2 * HALF, C), F32), pltpu.SemaphoreType.DMA((10,))],
        compiler_params=params(),
        cost_estimate=pl.CostEstimate(flops=5 * 10**9, bytes_accessed=10**7, transcendentals=0),
        name="tail",
    )(info, *operands)


def unpack_kernel(info, mine, other, parts, *refs):
    conv_out, outs, refs = refs[0], refs[1:5], refs[5:]
    halves, turned, held, full, arrive, leave = refs
    core = info[1]
    loads = [
        pltpu.make_async_copy(mine, halves.at[core], arrive.at[4]),
        pltpu.make_async_copy(other, halves.at[1 - core], arrive.at[5]),
    ]
    for which in range(4):
        at = slice(which * HD, (which + 1) * HD)
        loads.append(pltpu.make_async_copy(parts.at[:, at, :], held.at[which], arrive.at[which]))
    for load in loads:
        load.start()
    stores = [pltpu.make_async_copy(turned.at[tap], conv_out.at[tap], leave.at[4 + tap]) for tap in range(KW)]
    stores += [pltpu.make_async_copy(full.at[which], outs[which], leave.at[which]) for which in range(4)]
    loads[0].wait()
    loads[1].wait()
    rows = halves[...].reshape(2 * HALF, C)
    for tap in range(KW):
        turned[tap] = rows[tap * CG : (tap + 1) * CG, :].astype(F32).T.reshape(G, CG, CG)
        stores[tap].start()
    for which in range(4):
        loads[2 + which].wait()
        part = held[which].reshape(C, C).astype(F32)
        full[which] = part if which == 0 else part.T
        stores[KW + which].start()
    for store in stores:
        store.wait()


def unpack(info, mine, other, parts):
    return pl.pallas_call(
        unpack_kernel,
        out_shape=[jax.ShapeDtypeStruct((KW, G, CG, CG), F32)] + [jax.ShapeDtypeStruct((C, C), F32)] * 4,
        in_specs=[smem()] + [hbm()] * 3,
        out_specs=[hbm()] * 5,
        scratch_shapes=[
            pltpu.VMEM((2, HALF, C), BF),
            pltpu.VMEM((KW, G, CG, CG), F32),
            pltpu.VMEM((4, H, HD, C), BF),
            pltpu.VMEM((4, C, C), F32),
            pltpu.SemaphoreType.DMA((6,)),
            pltpu.SemaphoreType.DMA((4 + KW,)),
        ],
        compiler_params=params(),
        cost_estimate=pl.CostEstimate(flops=10**7, bytes_accessed=20 * 10**6, transcendentals=0),
        name="unpack",
    )(info, mine, other, parts)


SWAP = [(0, 1), (1, 0)]
SEQ = ("chip", "core")
ALL_CHIPS = ("dp", "chip")


def apart(axis, bit):
    return [(i, i ^ bit) for i in range(lax.axis_size(axis))]


def to_chips(x, axes):
    return lax.all_to_all(x, axes, 0, 0, tiled=True)


def body(tokens, dilation, w_stem, conv_w, w_query, w_key, w_value, w_out, cotangent):
    core = lax.axis_index("core")
    chip = lax.axis_index("chip")
    me = lax.axis_index(SEQ)
    step = jnp.where(core == 1, -dilation[0], dilation[0])
    info = jnp.stack([step, core, chip]).astype(jnp.int32)
    own_cot = cotangent[0]
    ga_t = lax.dot_general(w_out, own_cot, (((1,), (1,)), ((), ())), preferred_element_type=F32).astype(BF)
    letters = jnp.broadcast_to(tokens.reshape(1, BP, BP).astype(BF), (H, BP, BP))
    pieces = to_chips(jnp.concatenate([letters, ga_t.reshape(H, HD, BP)], axis=1), SEQ)
    taps = conv_w.transpose(1, 0, 2, 3)
    conv = jnp.stack(
        [
            jnp.pad(taps[group], ((0, 0), (64, 0), (64, 0)) if group % 2 else ((0, 0), (0, 64), (0, 64)))
            for group in range(G)
        ]
    ).reshape(G, KW * 256, 256)
    w_qkv = jnp.concatenate(
        [
            jnp.pad(lax.dynamic_slice_in_dim(w, me * HD, HD, 1), ((0, 0), (0, 128 - HD)))
            for w in (w_query, w_key, w_value)
        ],
        axis=1,
    )
    pieces, own_cot, conv, w_qkv, info = lax.optimization_barrier((pieces, own_cot, conv, w_qkv, info))
    cot = lax.all_gather(own_cot, SEQ, axis=0, tiled=True)
    hidden, pre_own, emb_own = front(info, pieces, w_stem, conv)
    hidden_other = lax.ppermute(hidden, "core", SWAP)
    mine, from_mine = heads(hidden, pieces, w_qkv)
    got_same = to_chips(mine, "chip")
    other, wgrad = heads(hidden_other, pieces, w_qkv, cot, mine, from_mine)
    other, wgrad, got_same = lax.optimization_barrier((other, wgrad, got_same))
    got_cross = to_chips(lax.ppermute(other, "core", SWAP), "chip")
    once = lax.ppermute(wgrad, "dp", apart("dp", 1))
    wgrad = (wgrad.astype(F32) + once.astype(F32)).astype(BF)
    twice = lax.ppermute(wgrad, "dp", apart("dp", 2))
    twice, got_cross = lax.optimization_barrier((twice, got_cross))
    wgrad = (wgrad.astype(F32) + twice.astype(F32)).astype(BF)
    thrice = lax.ppermute(wgrad, "dp", apart("dp", 4))
    out_keep, out_give, conv_keep, conv_give = tail(
        info, got_same, got_cross, hidden, cot, w_out, w_query, w_key, w_value, pre_own, emb_own
    )
    thrice, conv_give, out_give = lax.optimization_barrier((thrice, conv_give, out_give))
    wgrad = (wgrad.astype(F32) + thrice.astype(F32)).astype(BF)
    wgrads = lax.all_gather(wgrad, SEQ, axis=0)
    conv_taken = lax.ppermute(conv_give, "core", SWAP)
    share = (conv_keep.astype(F32) + conv_taken.astype(F32)).astype(BF)
    parts = to_chips(share, ALL_CHIPS).reshape(64, HALF // 64, C)
    share = jnp.sum(parts.astype(F32), axis=0).astype(BF)
    conv_mine = to_chips(jnp.broadcast_to(share[None], (64, HALF // 64, C)), ALL_CHIPS).reshape(HALF, C)
    taken = lax.ppermute(out_give, "core", SWAP)
    mixed = (out_keep.astype(F32) + taken.astype(F32)).astype(BF)[None]
    conv_mine, mixed = lax.optimization_barrier((conv_mine, mixed))
    grad_conv, grad_out, grad_query, grad_key, grad_value = unpack(
        info, conv_mine, lax.ppermute(conv_mine, "core", SWAP), wgrads
    )
    return (mixed, grad_conv, grad_query, grad_key, grad_value, grad_out)


def solution(mesh):
    split = jax.sharding.Mesh(mesh.devices.reshape(8, 8, 2), ("dp", "chip", "core"))
    in_specs = (P("dp", SEQ), P("dp"), P(), P(), P(), P(), P(), P(), P("dp", SEQ, None))
    out_specs = (P("dp", SEQ, None), P(), P(), P(), P(), P())
    return jax.shard_map(body, mesh=split, in_specs=in_specs, out_specs=out_specs, check_vma=False)
```
